32 devices in a mesh: group: 16 (over z, y, x), member: 2 (over core).
Axes of the slice: x: 2, y: 2, z: 4, core: 2. Of those that a mesh axis runs over, the one named last changes fastest.
Arguments:
- residual: float32 [2, 256, 64, 128], P(None, 'group', 'member'), may hold values from -6 to 6
- horiz_vectors: float32 [2, 18, 18], replicated, may hold values from -1.5 to 1.5
- horiz_values: float32 [2, 18], replicated, may hold values from 0.2 to 4
- upward_eigen_tables: float32 [8, 18, 18], replicated, may hold values from -1.5 to 1.5
- upward_eigen_values: float32 [8, 18], replicated, may hold values from 0.2 to 4
- aggregate_map: int32 [16, 4, 8], P('group', 'member'), may hold values from 0 to 127, as said below
- coarse_inverse: float32 [128, 128], P('group', 'member')
Outputs:
- preconditioned: float32 [2, 256, 64, 128], P(None, 'group', 'member')
The draws below stay inside these ranges and needn't reach their ends.
Inputs may be any that keep to these rules, and one draw needn't show every extreme that they name: `aggregate_map`: the aggregate of each element; an element's aggregate holds elements next to it; every aggregate holds some element.
All inputs are finite; a program needn't handle non-finite values.
Results may differ from the reference program's by a relative error of at most 0.0003.
Values sent between devices are 32-bit elements; how exact they have to be, the bound alone decides.
A program may use at most 64 MiB of HBM per device.

```python
import math
import jax
import jax.numpy as jnp
from jax import lax

ELEMENT_POINTS = 16
EXTENDED_POINTS = 18
VECTOR_TOTAL = 2
ELEMENTS_FIRST = 16
ELEMENTS_SECOND = 4
ELEMENTS_UPWARD = 8
NX = 256
NY = 64
NZ = 128
NC = 128


def draw_aggregate_map(key, part):
    mesh_layout = (ELEMENTS_FIRST, ELEMENTS_SECOND, ELEMENTS_UPWARD)
    index_x = lax.broadcasted_iota(jnp.int32, mesh_layout, 0)
    index_y = lax.broadcasted_iota(jnp.int32, mesh_layout, 1)
    upward_index = lax.broadcasted_iota(jnp.int32, mesh_layout, 2)
    key_move = jax.random.fold_in(key, 11)
    key_side = jax.random.fold_in(key, 23)
    key_order = jax.random.fold_in(key, 37)
    moving = jax.random.randint(key_move, mesh_layout, 0, 4) == 0
    anchored = (index_x % 2 == 0) & (index_y % 2 == 0)
    moving = moving & jnp.logical_not(anchored)
    side = jax.random.randint(key_side, mesh_layout, 0, 4)
    step_x = jnp.where(side == 0, 1, jnp.where(side == 1, -1, 0)).astype(jnp.int32)
    step_y = jnp.where(side == 2, 1, jnp.where(side == 3, -1, 0)).astype(jnp.int32)
    step_x = jnp.where(moving, step_x, 0)
    step_y = jnp.where(moving, step_y, 0)
    shifted_first = (index_x + step_x + ELEMENTS_FIRST) % ELEMENTS_FIRST
    shifted_second = (index_y + step_y + ELEMENTS_SECOND) % ELEMENTS_SECOND
    base_label = (shifted_first // 2 * (ELEMENTS_SECOND // 2) * ELEMENTS_UPWARD + shifted_second // 2 * ELEMENTS_UPWARD + upward_index).astype(jnp.int32)
    numbering = jax.random.permutation(key_order, NC).astype(jnp.int32)
    return jnp.take(numbering, base_label.reshape(-1)).reshape(mesh_layout).astype(jnp.int32)


def draw_coarse_inverse(key, part):
    key_off = jax.random.fold_in(key, 5)
    key_diag = jax.random.fold_in(key, 7)
    spread = 6.0 / math.sqrt(NC)
    off_part = jnp.clip(jax.random.normal(key_off, (NC, NC), jnp.float32), -4.0, 4.0) * spread
    diag_part = jax.random.uniform(key_diag, (NC,), jnp.float32, 4.0, 8.0)
    row_index = lax.broadcasted_iota(jnp.int32, (NC, NC), 0)
    col_index = lax.broadcasted_iota(jnp.int32, (NC, NC), 1)
    return off_part + jnp.where(row_index == col_index, diag_part[:, None], 0.0).astype(jnp.float32)


def block_levels(stream_key, shape, cuts, low, high):
    loudness = 1.0
    for dim, shards_of in cuts:
        heights = jax.random.uniform(jax.random.fold_in(jax.random.fold_in(stream_key, 6), dim), (shards_of,), jnp.float32, low / len(cuts), high / len(cuts))
        loudness = loudness * jnp.repeat(jnp.exp(heights), shape[dim] // shards_of).reshape((-1,) + (1,) * (len(shape) - 1 - dim))
    return loudness


def centred(own_key, dims, deviation, bound, split=(), kind=jnp.bfloat16):
    array = deviation * jax.random.normal(own_key, dims, jnp.float32)
    if split:
        array = array * block_levels(own_key, dims, split, -0.22, 0.18)
    return jnp.clip(array, -bound, bound).astype(kind)


def setup_inputs(seed: int = 0) -> dict:
    key_list = jax.random.split(jax.random.key(seed), 8)
    return {
        "residual": centred(key_list[0], (VECTOR_TOTAL, NX, NY, NZ), 1.0, 6.0, ((1, 16), (2, 2)), jnp.float32),
        "horiz_vectors": centred(key_list[1], (2, EXTENDED_POINTS, EXTENDED_POINTS), EXTENDED_POINTS ** -0.5, 1.5, (), jnp.float32),
        "horiz_values": jnp.clip(jnp.exp(jax.random.uniform(key_list[2], (2, EXTENDED_POINTS), jnp.float32, math.log(0.2), math.log(4.0))), 0.2, 4.0),
        "upward_eigen_tables": centred(key_list[3], (ELEMENTS_UPWARD, EXTENDED_POINTS, EXTENDED_POINTS), EXTENDED_POINTS ** -0.5, 1.5, (), jnp.float32),
        "upward_eigen_values": jnp.clip(jnp.exp(jax.random.uniform(key_list[4], (ELEMENTS_UPWARD, EXTENDED_POINTS), jnp.float32, math.log(0.2), math.log(4.0))), 0.2, 4.0),
        "aggregate_map": draw_aggregate_map(jax.random.fold_in(key_list[7], 71), 0),
        "coarse_inverse": draw_coarse_inverse(jax.random.fold_in(key_list[7], 71), 0),
    }


def element_frames(field_in, along_axis, pieces, span):
    core_part = lax.slice_in_dim(field_in, 1, 1 + pieces * span, axis=along_axis)
    new_shape = core_part.shape[:along_axis] + (pieces, span) + core_part.shape[along_axis + 1:]
    core_part = core_part.reshape(new_shape)
    left_rim = lax.slice_in_dim(field_in, 0, pieces * span, stride=span, axis=along_axis)
    right_rim = lax.slice_in_dim(field_in, span + 1, pieces * span + 2, stride=span, axis=along_axis)
    left_rim = jnp.expand_dims(left_rim, along_axis + 1)
    right_rim = jnp.expand_dims(right_rim, along_axis + 1)
    return jnp.concatenate([left_rim, core_part, right_rim], axis=along_axis + 1)


def fdm_solve(extended_box_field, horiz_vectors, horiz_values, upward_eigen_tables, upward_eigen_values):
    highest = lax.Precision.HIGHEST
    hat = jnp.einsum('vxjykz,xa->vajykz', extended_box_field, horiz_vectors[0], precision=highest)
    hat = jnp.einsum('vajykz,yb->vajbkz', hat, horiz_vectors[1], precision=highest)
    hat = jnp.einsum('vajbkz,kzc->vajbkc', hat, upward_eigen_tables, precision=highest)
    denominator = (horiz_values[0][:, None, None, None, None]
                   + horiz_values[1][None, None, :, None, None]
                   + upward_eigen_values[None, None, None, :, :])
    scaled = hat / denominator[None]
    solved = jnp.einsum('vajbkc,kzc->vajbkz', scaled, upward_eigen_tables, precision=highest)
    solved = jnp.einsum('vajbkz,yb->vajykz', solved, horiz_vectors[1], precision=highest)
    solved = jnp.einsum('vajykz,xa->vxjykz', solved, horiz_vectors[0], precision=highest)
    return solved[:, 1:-1, :, 1:-1, :, 1:-1]


def reference(residual, horiz_vectors, horiz_values, upward_eigen_tables, upward_eigen_values, aggregate_map, coarse_inverse):
    partition_weight = float(ELEMENT_POINTS) ** -1.5

    def slab_solve(index):
        rows_x = (index * ELEMENT_POINTS - 1 + jnp.arange(EXTENDED_POINTS, dtype=jnp.int32)) % NX
        layer_sheet = jnp.take(residual, rows_x.astype(jnp.int32), axis=1)
        layer_sheet = jnp.concatenate([layer_sheet[:, :, -1:], layer_sheet, layer_sheet[:, :, :1]], axis=2)
        layer_sheet = jnp.pad(layer_sheet, ((0, 0), (0, 0), (0, 0), (1, 1)))
        extended_box_field = element_frames(element_frames(layer_sheet, 2, ELEMENTS_SECOND, ELEMENT_POINTS), 4, ELEMENTS_UPWARD, ELEMENT_POINTS)
        solved = fdm_solve(extended_box_field, horiz_vectors, horiz_values, upward_eigen_tables, upward_eigen_values)
        return solved.reshape(VECTOR_TOTAL, ELEMENT_POINTS, NY, NZ)

    subdomain_part = lax.map(slab_solve, jnp.arange(ELEMENTS_FIRST, dtype=jnp.int32))
    subdomain_part = jnp.transpose(subdomain_part, (1, 0, 2, 3, 4)).reshape(VECTOR_TOTAL, NX, NY, NZ)

    element_totals = residual.reshape(VECTOR_TOTAL, ELEMENTS_FIRST, ELEMENT_POINTS, ELEMENTS_SECOND, ELEMENT_POINTS, ELEMENTS_UPWARD, ELEMENT_POINTS).sum(axis=(2, 4, 6))
    aggregate_labels = aggregate_map.reshape(-1).astype(jnp.int32)
    coarse_rhs = partition_weight * jax.ops.segment_sum(element_totals.reshape(VECTOR_TOTAL, -1).T, aggregate_labels, num_segments=NC).T
    coarse_answer = jnp.dot(coarse_rhs, coarse_inverse.T, precision=lax.Precision.HIGHEST,
                              preferred_element_type=jnp.float32)
    update_term = partition_weight * jnp.take(coarse_answer, aggregate_labels, axis=1).reshape(VECTOR_TOTAL, ELEMENTS_FIRST, ELEMENTS_SECOND, ELEMENTS_UPWARD)
    merged_result = subdomain_part.reshape(VECTOR_TOTAL, ELEMENTS_FIRST, ELEMENT_POINTS, ELEMENTS_SECOND, ELEMENT_POINTS, ELEMENTS_UPWARD, ELEMENT_POINTS) + update_term[:, :, None, :, None, :, None]
    return merged_result.reshape(VECTOR_TOTAL, NX, NY, NZ)
```

```python
import functools

import jax
import jax.numpy as jnp
from jax import lax
from jax.experimental import pallas as pl
from jax.experimental.pallas import tpu as pltpu
from jax.sharding import PartitionSpec as P

SPAN = 16
EXTENT = SPAN + 2
MAIN = SPAN * SPAN
TAIL = 24
REST = 2 * SPAN + 2 * TAIL
ROWS = MAIN + REST
WEIGHT = float(SPAN) ** (-1.5)
MESH = pl.DeviceIdType.MESH
F32 = jnp.float32
BF16 = jnp.bfloat16


def iota(shape, dim):
    return lax.broadcasted_iota(jnp.int32, shape, dim)


def dot(a, b):
    return jnp.dot(a, b, precision=lax.Precision.HIGHEST, preferred_element_type=F32)


def dot_t(a, b):
    dims = (((1,), (1,)), ((), ()))
    return lax.dot_general(
        a, b, dims, precision=lax.Precision.HIGHEST, preferred_element_type=F32
    )


def bdot(a, b):
    return jnp.dot(a, b, preferred_element_type=F32)


def split(a):
    hi = a.astype(BF16)
    return hi, (a - hi.astype(F32)).astype(BF16)


def rest_of(lane):
    r = lane - MAIN
    r = jnp.where(r >= 2 * REST, r - 2 * REST, jnp.where(r >= REST, r - REST, r))
    t = r - 2 * SPAN
    tail = (t >= 0) & (lane < MAIN + 3 * REST)
    second = t >= TAIL
    return r, tail, second, jnp.where(second, t - TAIL, t)


def point_index(lane):
    r, tail, second, along = rest_of(lane)
    side = jnp.where(r >= SPAN, EXTENT - 1, 0)
    tail_x = jnp.where(
        along < SPAN,
        along + 1,
        jnp.where(along == SPAN, 0, jnp.where(along == SPAN + 1, EXTENT - 1, -1)),
    )
    x = jnp.where(lane < MAIN, 1 + lane // SPAN, jnp.where(tail, tail_x, side))
    y = jnp.where(
        lane < MAIN,
        1 + lane % SPAN,
        jnp.where(tail, jnp.where(second, EXTENT - 1, 0), 1 + r % SPAN),
    )
    return x, y


def mode_index(lane):
    r, tail, second, along = rest_of(lane)
    a = jnp.where(lane < MAIN, lane // SPAN, jnp.where(tail, along, SPAN + r // SPAN))
    b = jnp.where(
        lane < MAIN,
        lane % SPAN,
        jnp.where(tail, jnp.where(second, SPAN + 1, SPAN), r % SPAN),
    )
    return a, b


def store_split(ref, table):
    hi, lo = split(table)
    rows = table.shape[0]
    ref[:, 0:MAIN] = hi[:, :MAIN]
    ref[:, MAIN : 2 * MAIN] = hi[:, :MAIN]
    ref[:, 2 * MAIN : 3 * MAIN] = lo[:, :MAIN]
    lane = iota((rows, MAIN), 1)
    wide = table[:, MAIN:]
    top = wide.astype(BF16).astype(F32)
    mixed = jnp.where(lane < 2 * REST, top, wide - top)
    ref[:, 3 * MAIN :] = jnp.where(lane < 3 * REST, mixed, 0.0).astype(BF16)


def kernel(
    groups,
    members,
    direct,
    res_hbm,
    hvec_hbm,
    hval_hbm,
    ztab_hbm,
    zval_hbm,
    agg_hbm,
    inv_hbm,
    out_hbm,
    res,
    hvec,
    hval,
    ztab,
    zval,
    agg,
    inv,
    out,
    hpad,
    zpad,
    apad,
    ysend,
    csend,
    xrecv,
    yrecv,
    crecv,
    msg,
    box,
    fwd,
    bwd,
    recip,
    zfwd,
    zbwd,
    part,
    in_sem,
    out_sem,
    halo_send,
    halo_recv,
    all_send,
    all_recv,
):
    vectors, _, span_y, span_z = res.shape
    count_y = span_y // SPAN
    count_z = span_z // SPAN
    modes_z = count_z * EXTENT
    total = groups * members
    g = lax.axis_index("group")
    m = lax.axis_index("member")
    me = g * members + m

    def peer(step):
        other = lax.rem(me + step, total)
        return (other // members, lax.rem(other, members))

    def shifted(dx, dy):
        return (lax.rem(g + dx + groups, groups), lax.rem(m + dy + members, members))

    barrier = pltpu.get_barrier_semaphore()
    around = [(dx, dy) for dx in (-1, 0, 1) for dy in (-1, 0, 1) if dx or dy]
    if direct:

        def greet(step, carry):
            pl.semaphore_signal(barrier, inc=1, device_id=peer(step), device_id_type=MESH)
            return carry

        lax.fori_loop(1, total, greet, 0)
    else:
        for dx, dy in around:
            pl.semaphore_signal(
                barrier, inc=1, device_id=shifted(dx, dy), device_id_type=MESH
            )

    loads = [
        pltpu.make_async_copy(src, dst, in_sem.at[i])
        for i, (src, dst) in enumerate(
            [
                (res_hbm, res),
                (agg_hbm, agg),
                (inv_hbm, inv),
                (hvec_hbm, hvec),
                (hval_hbm, hval),
                (ztab_hbm, ztab),
                (zval_hbm, zval),
            ]
        )
    ]
    for load in loads:
        load.start()
    hpad[...] = jnp.zeros_like(hpad)
    zpad[...] = jnp.zeros_like(zpad)
    apad[...] = jnp.zeros_like(apad)
    for load in loads:
        load.wait()

    for v in range(vectors):
        ysend[0, v] = res[v, :, span_y - 1, :]
        ysend[1, v] = res[v, :, 0, :]
    for cx in range(2):
        for cy in range(2):
            for v in range(vectors):
                row = cx * 4 + cy * 2 + v
                y_at = (span_y - 1) * cy
                csend[row : row + 1, :] = res[v, (SPAN - 1) * cx, y_at : y_at + 1, :]

    row8 = iota((8, span_z), 0)
    if direct:
        spread = (iota((count_z, span_z), 1) // SPAN == iota((count_z, span_z), 0)).astype(F32)
        labels = dot(agg[0].astype(F32), spread)
        half = inv.shape[1]
        row_id = iota((2 * half, span_z), 0)
        rhs = jnp.zeros((8, 2 * half), F32)
        for j in range(count_y):
            sums = jnp.zeros((8, span_z), F32)
            for v in range(vectors):
                tot = jnp.sum(res[v, :, j * SPAN : (j + 1) * SPAN, :], axis=0)
                tot = jnp.sum(tot, axis=0, keepdims=True)
                sums = sums + jnp.where(row8 % 4 == v, tot, 0.0)
            label = labels[j : j + 1, :]
            low = (label == (row_id - half).astype(F32)) & (row_id >= half)
            high = (label == row_id.astype(F32)) & (row_id >= half)
            rhs = rhs + jnp.where(
                row8 < 4, dot_t(sums, low.astype(F32)), dot_t(sums, high.astype(F32))
            )
        apad[:, 0:half] = inv[...]
        mine = apad[...] + WEIGHT * rhs
        msg[me] = mine
        box[...] = mine

    halo = []

    def send(src, dst, dx, dy):
        i = len(halo)
        copy = pltpu.make_async_remote_copy(
            src_ref=src,
            dst_ref=dst,
            send_sem=halo_send.at[i],
            recv_sem=halo_recv.at[i],
            device_id=shifted(dx, dy),
            device_id_type=MESH,
        )
        halo.append(copy)

    send(res.at[:, SPAN - 1], xrecv.at[0], 1, 0)
    send(res.at[:, 0], xrecv.at[1], -1, 0)
    corner_dy = (1,) if members == 2 else (1, -1)
    for ix, dx in enumerate((1, -1)):
        for iy, dy in enumerate(corner_dy):
            send(csend, crecv.at[ix, iy], dx, dy)
    send(ysend.at[0], yrecv.at[0], 0, 1)
    send(ysend.at[1], yrecv.at[1], 0, -1)

    pl.semaphore_wait(barrier, total - 1 if direct else len(around))
    for copy in halo:
        copy.start()
    if direct:

        def share(step, carry):
            pltpu.make_async_remote_copy(
                src_ref=box,
                dst_ref=msg.at[me],
                send_sem=all_send,
                recv_sem=all_recv,
                device_id=peer(step),
                device_id_type=MESH,
            ).start()
            return carry

        lax.fori_loop(1, total, share, 0)

    hpad[:, 0:EXTENT, 0:EXTENT] = hvec[...]
    wide = 2 * MAIN
    lane = iota((TAIL, wide), 1)
    row = iota((TAIL, wide), 0)
    eye = (iota((TAIL, 128), 0) == iota((TAIL, 128), 1)).astype(F32)
    px, py = point_index(lane)
    xe = dot(dot_t(eye, hpad[0]), (px == row).astype(F32))
    ye = dot(dot_t(eye, hpad[1]), (py == row).astype(F32))
    body = xe[:EXTENT][:, None, :] * ye[:SPAN][None, :, :]
    table = jnp.concatenate(
        [
            body.reshape(EXTENT * SPAN, wide),
            xe * ye[SPAN : SPAN + 1, :],
            xe * ye[SPAN + 1 : SPAN + 2, :],
        ],
        axis=0,
    )
    store_split(fwd, table)
    ma, mb = mode_index(lane)
    xb = dot(hpad[0, 1 : SPAN + 1, 0:TAIL], (ma == row).astype(F32))
    yb = dot(hpad[1, 1 : SPAN + 1, 0:TAIL], (mb == row).astype(F32))
    store_split(bwd, (xb[:, None, :] * yb[None, :, :]).reshape(MAIN, wide))

    zpad[:, 0:EXTENT, 0:EXTENT] = ztab[...]
    tiled = (iota((128, modes_z), 1) % EXTENT == iota((128, modes_z), 0)).astype(F32)
    stacked = count_z * TAIL
    diag = dot(zpad[...].reshape(stacked, 128), tiled)
    own = iota((stacked, modes_z), 1) // EXTENT == iota((stacked, modes_z), 0) // TAIL
    diag = jnp.where(own, diag, 0.0)
    zz = iota((span_z, stacked), 0)
    layer = iota((span_z, stacked), 1) // TAIL
    inner = iota((span_z, stacked), 1) % TAIL
    band = ((zz == SPAN * layer - 1 + inner) & (inner < EXTENT)).astype(F32)
    near = ((zz // SPAN == layer) & (inner == zz % SPAN + 1)).astype(F32)
    hi, lo = split(dot(band, diag))
    zfwd[0:span_z, :] = hi
    zfwd[span_z : 2 * span_z, :] = lo
    zfwd[2 * span_z : 3 * span_z, :] = hi
    eye_z = (iota((modes_z, modes_z), 0) == iota((modes_z, modes_z), 1)).astype(F32)
    hi, lo = split(dot_t(eye_z, dot(near, diag)))
    zbwd[:, 0:span_z] = hi
    zbwd[:, span_z : 2 * span_z] = lo

    lane_h = iota((ROWS, EXTENT), 1)
    row_h = iota((ROWS, EXTENT), 0)
    t = row_h - EXTENT * SPAN
    along = jnp.where(t >= TAIL, t - TAIL, t)
    a_of = jnp.where(t < 0, row_h // SPAN, along)
    b_of = jnp.where(t < 0, row_h % SPAN, jnp.where(t >= TAIL, SPAN + 1, SPAN))
    column = jnp.where(lane_h == a_of, hval[0:1, :], 0.0)
    column = column + jnp.where(lane_h == b_of, hval[1:2, :], 0.0)
    column = jnp.sum(column, axis=1, keepdims=True)
    levels = dot(zval[...], tiled[:EXTENT])
    level_own = iota((count_z, modes_z), 1) // EXTENT == iota((count_z, modes_z), 0)
    levels = jnp.sum(jnp.where(level_own, levels, 0.0), axis=0, keepdims=True)
    recip[...] = 1.0 / (column + levels)

    for v in range(vectors):
        field = jnp.concatenate(
            [
                res[v, :, j * SPAN : (j + 1) * SPAN, :].reshape(MAIN, span_z)
                for j in range(count_y)
            ],
            axis=1,
        )
        hi, lo = split(field)
        part[v] = bdot(fwd[:, 0 : 3 * MAIN], jnp.concatenate([hi, lo, hi], axis=0))

    for copy in halo:
        copy.wait_recv()

    rim_row = iota((8, span_z), 0)
    solved = []
    for v in range(vectors):
        rests = []
        for j in range(count_y):
            rows = slice(j * SPAN, (j + 1) * SPAN)
            pieces = [xrecv[0, v, rows, :], xrecv[1, v, rows, :]]
            for side in range(2):
                at = j * SPAN - 1 if side == 0 else (j + 1) * SPAN
                if 0 <= at < span_y:
                    pieces.append(res[v, :, at, :])
                    before = xrecv[0, v, at : at + 1, :]
                    after = xrecv[1, v, at : at + 1, :]
                else:
                    pieces.append(yrecv[side, v])
                    iy = 0 if members == 2 else side
                    cy = 1 - side
                    r0, r1 = 4 + cy * 2 + v, cy * 2 + v
                    before = crecv[0, iy, r0 : r0 + 1, :]
                    after = crecv[1, iy, r1 : r1 + 1, :]
                pieces.append(
                    jnp.where(rim_row == 0, before, jnp.where(rim_row == 1, after, 0.0))
                )
            rests.append(jnp.concatenate(pieces, axis=0))
        hi, lo = split(jnp.concatenate(rests, axis=1))
        hat = part[v] + bdot(fwd[:, 3 * MAIN :][:, : 3 * REST], jnp.concatenate([hi, lo, hi], axis=0))
        backs = []
        for j in range(count_y):
            hi, lo = split(hat[:, j * span_z : (j + 1) * span_z])
            spectral = bdot(jnp.concatenate([hi, hi, lo], axis=1), zfwd[...]) * recip[...]
            hi, lo = split(spectral)
            both = bdot(hi, zbwd[...])
            backs.append(
                both[:, :span_z] + both[:, span_z:] + bdot(lo, zbwd[:, 0:span_z])
            )
        solved.append(jnp.concatenate(backs, axis=1))

    updates = None
    if direct:
        done = pltpu.make_async_copy(
            msg.at[pl.ds(0, total - 1)], msg.at[pl.ds(0, total - 1)], all_recv
        )
        done.wait()
        blocks = msg[...]
        whole = pltpu.roll(jnp.sum(blocks, axis=0), half, 1)
        lane8 = iota((8, 2 * half), 1)
        whole = jnp.where(lane8 < half, whole, 0.0)
        blocks = blocks.reshape(groups, members, 8, 2 * half)
        answer = jnp.zeros((8, groups * 8), F32)
        for part_m in range(members):
            chosen = jnp.where(row8 // 4 == part_m, whole, 0.0)
            answer = answer + dot_t(chosen, blocks[:, part_m].reshape(groups * 8, 2 * half))
        updates = []
        for j in range(count_y):
            pick = (labels[j : j + 1, :] == row_id.astype(F32)).astype(F32)
            updates.append(WEIGHT * dot(answer, pick))

    stores = []
    for v in range(vectors):
        hi, lo = split(solved[v])
        result = bdot(
            bwd[:, 0 : 3 * MAIN],
            jnp.concatenate([hi[:MAIN], lo[:MAIN], hi[:MAIN]], axis=0),
        ) + bdot(
            bwd[:, 3 * MAIN :][:, : 3 * REST],
            jnp.concatenate([hi[MAIN:], lo[MAIN:], hi[MAIN:]], axis=0),
        )
        for j in range(count_y):
            piece = result[:, j * span_z : (j + 1) * span_z]
            if direct:
                piece = piece + (updates[j][v : v + 1, :] + updates[j][4 + v : 5 + v, :])
            out[v, :, j * SPAN : (j + 1) * SPAN, :] = piece.reshape(SPAN, SPAN, span_z)
        store = pltpu.make_async_copy(out.at[v], out_hbm.at[v], out_sem.at[v])
        store.start()
        stores.append(store)

    for copy in halo:
        copy.wait_send()
    if direct:
        pltpu.make_async_copy(
            msg.at[pl.ds(0, total - 1)], msg.at[pl.ds(0, total - 1)], all_send
        ).wait()
    for store in stores:
        store.wait()


def on_device(
    residual,
    horiz_vectors,
    horiz_values,
    upward_eigen_tables,
    upward_eigen_values,
    aggregate_map,
    coarse_inverse,
):
    groups = lax.axis_size("group")
    members = lax.axis_size("member")
    vectors, points_x, span_y, span_z = residual.shape
    count_y = span_y // SPAN
    count_z = span_z // SPAN
    total = groups * members
    rows, cols = coarse_inverse.shape
    direct = total <= 64 and members == 2 and rows == 8 and cols == 64 and groups * 8 == 128
    operands = (
        residual,
        horiz_vectors,
        horiz_values,
        upward_eigen_tables,
        upward_eigen_values,
        aggregate_map,
        coarse_inverse,
    )
    corners = 1 if members == 2 else 2
    halos = 4 + 2 * corners
    dma = pltpu.SemaphoreType.DMA
    scratch = [pltpu.VMEM(a.shape, a.dtype) for a in operands]
    scratch += [
        pltpu.VMEM(residual.shape, F32),
        pltpu.VMEM((2, TAIL, 128), F32),
        pltpu.VMEM((count_z, TAIL, 128), F32),
        pltpu.VMEM((8, 128), F32),
        pltpu.VMEM((2, vectors, SPAN, span_z), F32),
        pltpu.VMEM((8, span_z), F32),
        pltpu.VMEM((2, vectors, span_y, span_z), F32),
        pltpu.VMEM((2, vectors, SPAN, span_z), F32),
        pltpu.VMEM((2, corners, 8, span_z), F32),
        pltpu.VMEM((total if direct else 1, 8, 128), F32),
        pltpu.VMEM((8, 128), F32),
        pltpu.VMEM((ROWS, 4 * MAIN), BF16),
        pltpu.VMEM((MAIN, 4 * MAIN), BF16),
        pltpu.VMEM((ROWS, count_z * EXTENT), F32),
        pltpu.VMEM((3 * span_z, count_z * EXTENT), BF16),
        pltpu.VMEM((count_z * EXTENT, 2 * span_z), BF16),
        pltpu.VMEM((vectors, ROWS, count_y * span_z), F32),
        dma((len(operands),)),
        dma((vectors,)),
        dma((halos,)),
        dma((halos,)),
        dma,
        dma,
    ]
    result = pl.pallas_call(
        functools.partial(kernel, groups, members, direct),
        out_shape=jax.ShapeDtypeStruct(residual.shape, F32),
        in_specs=[pl.BlockSpec(memory_space=pl.ANY)] * len(operands),
        out_specs=pl.BlockSpec(memory_space=pl.ANY),
        scratch_shapes=scratch,
        compiler_params=pltpu.CompilerParams(
            collective_id=0, has_side_effects=True, vmem_limit_bytes=40 * 1024 * 1024
        ),
        cost_estimate=pl.CostEstimate(
            flops=2 * 10**9, bytes_accessed=2**20, transcendentals=0
        ),
    )(*operands)
    if direct:
        return result
    totals = residual.reshape(vectors, SPAN, count_y, SPAN, count_z, SPAN).sum(axis=(1, 3, 5))
    labels = aggregate_map.reshape(-1)
    partial_rhs = WEIGHT * jax.ops.segment_sum(
        totals.reshape(vectors, -1).T, labels, num_segments=rows * groups
    ).T
    whole_rhs = lax.psum(partial_rhs, ("group", "member"))
    share = lax.dynamic_slice_in_dim(whole_rhs, lax.axis_index("member") * cols, cols, 1)
    row_values = lax.psum(dot(share, coarse_inverse.T), "member")
    coarse = lax.all_gather(row_values, "group", axis=1, tiled=True)
    update = WEIGHT * jnp.take(coarse, labels, axis=1)
    update = update.reshape(vectors, 1, count_y, 1, count_z, 1)
    split_up = (vectors, SPAN, count_y, SPAN, count_z, SPAN)
    return (result.reshape(split_up) + update).reshape(residual.shape)


def solution(mesh):
    in_specs = (
        P(None, "group", "member", None),
        P(),
        P(),
        P(),
        P(),
        P("group", "member", None),
        P("group", "member"),
    )
    out_specs = P(None, "group", "member", None)
    return jax.shard_map(
        on_device, mesh=mesh, in_specs=in_specs, out_specs=out_specs, check_vma=False
    )
```

```python
import functools

import jax
import jax.numpy as jnp
from jax import lax
from jax.experimental import pallas as pl
from jax.experimental.pallas import tpu as pltpu
from jax.sharding import PartitionSpec as P

SPAN = 16
EXTENT = SPAN + 2
MAIN = SPAN * SPAN
TAIL = 24
REST = 2 * SPAN + 2 * TAIL
ROWS = MAIN + REST
WEIGHT = float(SPAN) ** (-1.5)
MESH = pl.DeviceIdType.MESH
F32 = jnp.float32
BF16 = jnp.bfloat16


def iota(shape, dim):
    return lax.broadcasted_iota(jnp.int32, shape, dim)


def dot(a, b):
    return jnp.dot(a, b, precision=lax.Precision.HIGHEST, preferred_element_type=F32)


def dot_t(a, b):
    dims = (((1,), (1,)), ((), ()))
    return lax.dot_general(
        a, b, dims, precision=lax.Precision.HIGHEST, preferred_element_type=F32
    )


def bdot(a, b):
    return jnp.dot(a, b, preferred_element_type=F32)


def bdot_t(a, b):
    dims = (((1,), (1,)), ((), ()))
    return lax.dot_general(a, b, dims, preferred_element_type=F32)


def split(a):
    hi = a.astype(BF16)
    return hi, (a - hi.astype(F32)).astype(BF16)


def choose(a, hot):
    hi, lo = split(a)
    return bdot(hi, hot) + bdot(lo, hot)


def place(hot, a):
    hi, lo = split(a)
    return bdot(hot, hi) + bdot(hot, lo)


def turn(hot, a):
    hi, lo = split(a)
    return bdot_t(hot, hi) + bdot_t(hot, lo)


def hot(condition):
    return condition.astype(F32).astype(BF16)


def high(i):
    return lax.shift_right_logical(i, 4)


def low(i):
    return i & (SPAN - 1)


def rest_of(lane):
    r = lane - MAIN
    r = jnp.where(r >= 2 * REST, r - 2 * REST, jnp.where(r >= REST, r - REST, r))
    t = r - 2 * SPAN
    tail = (t >= 0) & (lane < MAIN + 3 * REST)
    second = t >= TAIL
    return r, tail, second, jnp.where(second, t - TAIL, t)


def point_index(lane):
    r, tail, second, along = rest_of(lane)
    side = jnp.where(r >= SPAN, EXTENT - 1, 0)
    tail_x = jnp.where(
        along < SPAN,
        along + 1,
        jnp.where(along == SPAN, 0, jnp.where(along == SPAN + 1, EXTENT - 1, -1)),
    )
    x = jnp.where(lane < MAIN, 1 + high(lane), jnp.where(tail, tail_x, side))
    y = jnp.where(
        lane < MAIN,
        1 + low(lane),
        jnp.where(tail, jnp.where(second, EXTENT - 1, 0), 1 + low(r)),
    )
    return x, y


def mode_index(lane):
    r, tail, second, along = rest_of(lane)
    a = jnp.where(lane < MAIN, high(lane), jnp.where(tail, along, SPAN + high(r)))
    b = jnp.where(
        lane < MAIN,
        low(lane),
        jnp.where(tail, jnp.where(second, SPAN + 1, SPAN), low(r)),
    )
    return a, b


def store_split(ref, table):
    hi, lo = split(table)
    rows = table.shape[0]
    ref[:, 0:MAIN] = hi[:, :MAIN]
    ref[:, MAIN : 2 * MAIN] = hi[:, :MAIN]
    ref[:, 2 * MAIN : 3 * MAIN] = lo[:, :MAIN]
    lane = iota((rows, MAIN), 1)
    wide = table[:, MAIN:]
    top = wide.astype(BF16).astype(F32)
    mixed = jnp.where(lane < 2 * REST, top, wide - top)
    ref[:, 3 * MAIN :] = jnp.where(lane < 3 * REST, mixed, 0.0).astype(BF16)


def kernel(
    groups,
    members,
    direct,
    res_hbm,
    hvec_hbm,
    hval_hbm,
    ztab_hbm,
    zval_hbm,
    agg_hbm,
    inv_hbm,
    out_hbm,
    res,
    hvec,
    hval,
    ztab,
    zval,
    agg,
    inv,
    out,
    hpad,
    apad,
    ysend,
    csend,
    xrecv,
    yrecv,
    crecv,
    msg,
    box,
    fwd,
    bwd,
    recip,
    zfwd,
    zbwd,
    part,
    in_sem,
    out_sem,
    halo_send,
    halo_recv,
    all_send,
    all_recv,
):
    vectors, _, span_y, span_z = res.shape
    count_y = span_y // SPAN
    count_z = span_z // SPAN
    modes_z = count_z * EXTENT
    total = groups * members
    g = lax.axis_index("group")
    m = lax.axis_index("member")
    me = g * members + m

    def wrap(i, n):
        return jnp.where(i >= n, i - n, i)

    def shifted(dx, dy):
        return (wrap(g + dx % groups, groups), wrap(m + dy % members, members))

    def for_peers(act):
        for dy in range(1, members):
            act(shifted(0, dy))

        def step(dx, carry):
            other = wrap(g + dx, groups)
            for dy in range(members):
                act((other, wrap(m + dy, members)))
            return carry

        lax.fori_loop(1, groups, step, 0)

    barrier = pltpu.get_barrier_semaphore()
    around = [(dx, dy) for dx in (-1, 0, 1) for dy in (-1, 0, 1) if dx or dy]
    if direct:
        for_peers(
            lambda device: pl.semaphore_signal(
                barrier, inc=1, device_id=device, device_id_type=MESH
            )
        )
    else:
        for dx, dy in around:
            pl.semaphore_signal(
                barrier, inc=1, device_id=shifted(dx, dy), device_id_type=MESH
            )

    loads = [
        pltpu.make_async_copy(src, dst, in_sem.at[i])
        for i, (src, dst) in enumerate(
            [
                (res_hbm, res),
                (agg_hbm, agg),
                (inv_hbm, inv),
                (hvec_hbm, hvec),
                (hval_hbm, hval),
                (ztab_hbm, ztab),
                (zval_hbm, zval),
            ]
        )
    ]
    for load in loads:
        load.start()
    hpad[...] = jnp.zeros_like(hpad)
    apad[...] = jnp.zeros_like(apad)
    for load in loads[1:]:
        load.wait()

    hpad[0, 0:EXTENT, 0:EXTENT] = hvec[:, 0, :]
    hpad[1, 0:EXTENT, 0:EXTENT] = hvec[:, 1, :]
    wide = 2 * MAIN
    lane = iota((1, wide), 1)
    row = iota((TAIL, wide), 0)
    eye = hot(iota((TAIL, 128), 0) == iota((TAIL, 128), 1))
    px, py = point_index(lane)
    xe = choose(turn(eye, hpad[0]), hot(px == row))
    ye = choose(turn(eye, hpad[1]), hot(py == row))
    body = xe[:EXTENT][:, None, :] * ye[:SPAN][None, :, :]
    table = jnp.concatenate(
        [
            body.reshape(EXTENT * SPAN, wide),
            xe * ye[SPAN : SPAN + 1, :],
            xe * ye[SPAN + 1 : SPAN + 2, :],
        ],
        axis=0,
    )
    store_split(fwd, table)
    ma, mb = mode_index(lane)
    xb = choose(hpad[0, 1 : SPAN + 1, 0:TAIL], hot(ma == row))
    yb = choose(hpad[1, 1 : SPAN + 1, 0:TAIL], hot(mb == row))
    store_split(bwd, (xb[:, None, :] * yb[None, :, :]).reshape(MAIN, wide))

    row8 = iota((8, span_z), 0)
    if direct:
        half = inv.shape[1]
        spread = hot(high(iota((count_z, span_z), 1)) == iota((count_z, span_z), 0))
        labels = dot(agg[0].astype(F32), spread.astype(F32))
        row_id = iota((2 * half, span_z), 0).astype(F32)
        member_of = jnp.concatenate(
            [hot(labels[j : j + 1, :] == row_id) for j in range(count_y)], axis=1
        )
        apad[:, 0:half] = inv[...]
    loads[0].wait()

    for v in range(vectors):
        ysend[0, v] = res[v, :, span_y - 1, :]
        ysend[1, v] = res[v, :, 0, :]
    for cx in range(2):
        for cy in range(2):
            for v in range(vectors):
                row = cx * 4 + cy * 2 + v
                y_at = (span_y - 1) * cy
                csend[row : row + 1, :] = res[v, (SPAN - 1) * cx, y_at : y_at + 1, :]

    if direct:
        sums = []
        for j in range(count_y):
            placed = jnp.zeros((8, span_z), F32)
            for v in range(vectors):
                tot = jnp.sum(res[v, :, j * SPAN : (j + 1) * SPAN, :], axis=0)
                tot = jnp.sum(tot, axis=0, keepdims=True)
                placed = placed + jnp.where((row8 & 3) == v, tot, 0.0)
            sums.append(placed)
        hi, lo = split(jnp.concatenate(sums, axis=1))
        rhs = WEIGHT * (bdot_t(hi, member_of) + bdot_t(lo, member_of))
        lane8 = iota((8, 2 * half), 1)
        rhs = jnp.where(row8 < 4, pltpu.roll(rhs, half, 1), rhs)
        mine = apad[...] + jnp.where(lane8 < half, 0.0, rhs)
        msg[me] = mine
        box[...] = mine

    halo = []

    def send(src, dst, dx, dy):
        i = len(halo)
        copy = pltpu.make_async_remote_copy(
            src_ref=src,
            dst_ref=dst,
            send_sem=halo_send.at[i],
            recv_sem=halo_recv.at[i],
            device_id=shifted(dx, dy),
            device_id_type=MESH,
        )
        halo.append(copy)

    send(res.at[:, SPAN - 1], xrecv.at[0], 1, 0)
    send(res.at[:, 0], xrecv.at[1], -1, 0)
    corner_dy = (1,) if members == 2 else (1, -1)
    for ix, dx in enumerate((1, -1)):
        for iy, dy in enumerate(corner_dy):
            send(csend, crecv.at[ix, iy], dx, dy)
    send(ysend.at[0], yrecv.at[0], 0, 1)
    send(ysend.at[1], yrecv.at[1], 0, -1)

    pl.semaphore_wait(barrier, total - 1 if direct else len(around))
    for copy in halo:
        copy.start()
    if direct:
        for_peers(
            lambda device: pltpu.make_async_remote_copy(
                src_ref=box,
                dst_ref=msg.at[me],
                send_sem=all_send,
                recv_sem=all_recv,
                device_id=device,
                device_id_type=MESH,
            ).start()
        )

    stacked = count_z * EXTENT
    mode = iota((1, modes_z), 1)
    mode_layer = mode // EXTENT
    mode_inner = mode - EXTENT * mode_layer
    tiled = hot(mode_inner == iota((EXTENT, modes_z), 0))
    diag = choose(ztab[...].reshape(stacked, EXTENT), tiled)
    diag = jnp.where(mode_layer == iota((stacked, modes_z), 0) % count_z, diag, 0.0)
    zz = iota((span_z, stacked), 0)
    layer = iota((1, stacked), 1) % count_z
    inner = iota((1, stacked), 1) // count_z
    band = hot(zz == SPAN * layer - 1 + inner)
    near = hot((high(zz) == layer) & (inner == low(zz) + 1))
    hi, lo = split(place(band, diag))
    zfwd[0:span_z, :] = hi
    zfwd[span_z : 2 * span_z, :] = lo
    zfwd[2 * span_z : 3 * span_z, :] = hi
    eye_z = hot(iota((modes_z, modes_z), 0) == iota((modes_z, modes_z), 1))
    hi, lo = split(turn(eye_z, place(near, diag)))
    zbwd[:, 0:span_z] = hi
    zbwd[:, span_z : 2 * span_z] = lo

    lane_h = iota((ROWS, EXTENT), 1)
    row_h = iota((ROWS, EXTENT), 0)
    t = row_h - EXTENT * SPAN
    along = jnp.where(t >= TAIL, t - TAIL, t)
    a_of = jnp.where(t < 0, high(row_h), along)
    b_of = jnp.where(t < 0, low(row_h), jnp.where(t >= TAIL, SPAN + 1, SPAN))
    column = jnp.where(lane_h == a_of, hval[0:1, :], 0.0)
    column = column + jnp.where(lane_h == b_of, hval[1:2, :], 0.0)
    column = jnp.sum(column, axis=1, keepdims=True)
    levels = dot(zval[...], tiled.astype(F32))
    level_own = mode_layer == iota((count_z, modes_z), 0)
    levels = jnp.sum(jnp.where(level_own, levels, 0.0), axis=0, keepdims=True)
    recip[...] = 1.0 / (column + levels)

    for v in range(vectors):
        field = jnp.concatenate(
            [
                res[v, :, j * SPAN : (j + 1) * SPAN, :].reshape(MAIN, span_z)
                for j in range(count_y)
            ],
            axis=1,
        )
        hi, lo = split(field)
        part[v] = bdot(fwd[:, 0 : 3 * MAIN], jnp.concatenate([hi, lo, hi], axis=0))

    for copy in halo:
        copy.wait_recv()

    rim_row = iota((8, span_z), 0)
    solved = []
    for v in range(vectors):
        rests = []
        for j in range(count_y):
            rows = slice(j * SPAN, (j + 1) * SPAN)
            pieces = [xrecv[0, v, rows, :], xrecv[1, v, rows, :]]
            for side in range(2):
                at = j * SPAN - 1 if side == 0 else (j + 1) * SPAN
                if 0 <= at < span_y:
                    pieces.append(res[v, :, at, :])
                    before = xrecv[0, v, at : at + 1, :]
                    after = xrecv[1, v, at : at + 1, :]
                else:
                    pieces.append(yrecv[side, v])
                    iy = 0 if members == 2 else side
                    cy = 1 - side
                    r0, r1 = 4 + cy * 2 + v, cy * 2 + v
                    before = crecv[0, iy, r0 : r0 + 1, :]
                    after = crecv[1, iy, r1 : r1 + 1, :]
                pieces.append(
                    jnp.where(rim_row == 0, before, jnp.where(rim_row == 1, after, 0.0))
                )
            rests.append(jnp.concatenate(pieces, axis=0))
        hi, lo = split(jnp.concatenate(rests, axis=1))
        hat = part[v] + bdot(fwd[:, 3 * MAIN :][:, : 3 * REST], jnp.concatenate([hi, lo, hi], axis=0))
        backs = []
        for j in range(count_y):
            hi, lo = split(hat[:, j * span_z : (j + 1) * span_z])
            spectral = bdot(jnp.concatenate([hi, hi, lo], axis=1), zfwd[...]) * recip[...]
            hi, lo = split(spectral)
            both = bdot(hi, zbwd[...])
            backs.append(
                both[:, :span_z] + both[:, span_z:] + bdot(lo, zbwd[:, 0:span_z])
            )
        solved.append(jnp.concatenate(backs, axis=1))

    updates = None
    if direct:
        done = pltpu.make_async_copy(
            msg.at[pl.ds(0, total - 1)], msg.at[pl.ds(0, total - 1)], all_recv
        )
        done.wait()
        blocks = msg[...]
        whole = pltpu.roll(jnp.sum(blocks, axis=0), half, 1)
        whole = jnp.where(lane8 < half, whole, 0.0)
        blocks = blocks.reshape(groups, members, 8, 2 * half)
        answer = jnp.zeros((8, groups * 8), F32)
        for part_m in range(members):
            chosen = jnp.where(row8 // 4 == part_m, whole, 0.0)
            answer = answer + dot_t(chosen, blocks[:, part_m].reshape(groups * 8, 2 * half))
        updates = WEIGHT * choose(answer, member_of)

    stores = []
    for v in range(vectors):
        hi, lo = split(solved[v])
        result = bdot(
            bwd[:, 0 : 3 * MAIN],
            jnp.concatenate([hi[:MAIN], lo[:MAIN], hi[:MAIN]], axis=0),
        ) + bdot(
            bwd[:, 3 * MAIN :][:, : 3 * REST],
            jnp.concatenate([hi[MAIN:], lo[MAIN:], hi[MAIN:]], axis=0),
        )
        for j in range(count_y):
            piece = result[:, j * span_z : (j + 1) * span_z]
            if direct:
                lanes = slice(j * span_z, (j + 1) * span_z)
                piece = piece + (updates[v : v + 1, lanes] + updates[4 + v : 5 + v, lanes])
            out[v, :, j * SPAN : (j + 1) * SPAN, :] = piece.reshape(SPAN, SPAN, span_z)
        store = pltpu.make_async_copy(out.at[v], out_hbm.at[v], out_sem.at[v])
        store.start()
        stores.append(store)

    for copy in halo:
        copy.wait_send()
    if direct:
        pltpu.make_async_copy(
            msg.at[pl.ds(0, total - 1)], msg.at[pl.ds(0, total - 1)], all_send
        ).wait()
    for store in stores:
        store.wait()


def on_device(
    residual,
    horiz_vectors,
    horiz_values,
    upward_eigen_tables,
    upward_eigen_values,
    aggregate_map,
    coarse_inverse,
):
    groups = lax.axis_size("group")
    members = lax.axis_size("member")
    vectors, points_x, span_y, span_z = residual.shape
    count_y = span_y // SPAN
    count_z = span_z // SPAN
    total = groups * members
    rows, cols = coarse_inverse.shape
    direct = total <= 64 and members == 2 and rows == 8 and cols == 64 and groups * 8 == 128
    operands = (
        residual,
        jnp.transpose(horiz_vectors, (1, 0, 2)),
        horiz_values,
        jnp.transpose(upward_eigen_tables, (1, 0, 2)),
        upward_eigen_values,
        aggregate_map,
        coarse_inverse,
    )
    corners = 1 if members == 2 else 2
    halos = 4 + 2 * corners
    dma = pltpu.SemaphoreType.DMA
    scratch = [pltpu.VMEM(a.shape, a.dtype) for a in operands]
    scratch += [
        pltpu.VMEM(residual.shape, F32),
        pltpu.VMEM((2, TAIL, 128), F32),
        pltpu.VMEM((8, 128), F32),
        pltpu.VMEM((2, vectors, SPAN, span_z), F32),
        pltpu.VMEM((8, span_z), F32),
        pltpu.VMEM((2, vectors, span_y, span_z), F32),
        pltpu.VMEM((2, vectors, SPAN, span_z), F32),
        pltpu.VMEM((2, corners, 8, span_z), F32),
        pltpu.VMEM((total if direct else 1, 8, 128), F32),
        pltpu.VMEM((8, 128), F32),
        pltpu.VMEM((ROWS, 4 * MAIN), BF16),
        pltpu.VMEM((MAIN, 4 * MAIN), BF16),
        pltpu.VMEM((ROWS, count_z * EXTENT), F32),
        pltpu.VMEM((3 * span_z, count_z * EXTENT), BF16),
        pltpu.VMEM((count_z * EXTENT, 2 * span_z), BF16),
        pltpu.VMEM((vectors, ROWS, count_y * span_z), F32),
        dma((len(operands),)),
        dma((vectors,)),
        dma((halos,)),
        dma((halos,)),
        dma,
        dma,
    ]
    result = pl.pallas_call(
        functools.partial(kernel, groups, members, direct),
        out_shape=jax.ShapeDtypeStruct(residual.shape, F32),
        in_specs=[pl.BlockSpec(memory_space=pltpu.HBM)] * len(operands),
        out_specs=pl.BlockSpec(memory_space=pl.ANY),
        scratch_shapes=scratch,
        compiler_params=pltpu.CompilerParams(
            collective_id=0, has_side_effects=True, vmem_limit_bytes=60 * 1024 * 1024
        ),
        cost_estimate=pl.CostEstimate(
            flops=2 * 10**9, bytes_accessed=2**20, transcendentals=0
        ),
    )(*operands)
    if direct:
        return result
    totals = residual.reshape(vectors, SPAN, count_y, SPAN, count_z, SPAN).sum(axis=(1, 3, 5))
    labels = aggregate_map.reshape(-1)
    partial_rhs = WEIGHT * jax.ops.segment_sum(
        totals.reshape(vectors, -1).T, labels, num_segments=rows * groups
    ).T
    whole_rhs = lax.psum(partial_rhs, ("group", "member"))
    share = lax.dynamic_slice_in_dim(whole_rhs, lax.axis_index("member") * cols, cols, 1)
    row_values = lax.psum(dot(share, coarse_inverse.T), "member")
    coarse = lax.all_gather(row_values, "group", axis=1, tiled=True)
    update = WEIGHT * jnp.take(coarse, labels, axis=1)
    update = update.reshape(vectors, 1, count_y, 1, count_z, 1)
    split_up = (vectors, SPAN, count_y, SPAN, count_z, SPAN)
    return (result.reshape(split_up) + update).reshape(residual.shape)


def solution(mesh):
    in_specs = (
        P(None, "group", "member", None),
        P(),
        P(),
        P(),
        P(),
        P("group", "member", None),
        P("group", "member"),
    )
    out_specs = P(None, "group", "member", None)
    return jax.shard_map(
        on_device, mesh=mesh, in_specs=in_specs, out_specs=out_specs, check_vma=False
    )
```

```python
import functools

import jax
import jax.numpy as jnp
from jax import lax
from jax.experimental import pallas as pl
from jax.experimental.pallas import tpu as pltpu
from jax.sharding import PartitionSpec as P

SPAN = 16
EXTENT = SPAN + 2
MAIN = SPAN * SPAN
TAIL = 24
REST = 2 * SPAN + 2 * TAIL
ROWS = MAIN + REST
WEIGHT = float(SPAN) ** (-1.5)
PLANES = 4
MESH = pl.DeviceIdType.MESH
F32 = jnp.float32
BF16 = jnp.bfloat16


def iota(shape, dim):
    return lax.broadcasted_iota(jnp.int32, shape, dim)


def dot(a, b):
    return jnp.dot(a, b, precision=lax.Precision.HIGHEST, preferred_element_type=F32)


def dot_t(a, b):
    dims = (((1,), (1,)), ((), ()))
    return lax.dot_general(
        a, b, dims, precision=lax.Precision.HIGHEST, preferred_element_type=F32
    )


def bdot(a, b):
    return jnp.dot(a, b, preferred_element_type=F32)


def bdot_t(a, b):
    dims = (((1,), (1,)), ((), ()))
    return lax.dot_general(a, b, dims, preferred_element_type=F32)


def split(a):
    hi = a.astype(BF16)
    return hi, (a - hi.astype(F32)).astype(BF16)


def choose(a, hot):
    hi, lo = split(a)
    return bdot(hi, hot) + bdot(lo, hot)


def place(hot, a):
    hi, lo = split(a)
    return bdot(hot, hi) + bdot(hot, lo)


def turn(hot, a):
    hi, lo = split(a)
    return bdot_t(hot, hi) + bdot_t(hot, lo)


def hot(condition):
    return condition.astype(F32).astype(BF16)


def high(i):
    return lax.shift_right_logical(i, 4)


def low(i):
    return i & (SPAN - 1)


def rest_of(lane):
    r = lane - MAIN
    r = jnp.where(r >= 2 * REST, r - 2 * REST, jnp.where(r >= REST, r - REST, r))
    t = r - 2 * SPAN
    tail = (t >= 0) & (lane < MAIN + 3 * REST)
    second = t >= TAIL
    return r, tail, second, jnp.where(second, t - TAIL, t)


def point_index(lane):
    r, tail, second, along = rest_of(lane)
    side = jnp.where(r >= SPAN, EXTENT - 1, 0)
    tail_x = jnp.where(
        along < SPAN,
        along + 1,
        jnp.where(along == SPAN, 0, jnp.where(along == SPAN + 1, EXTENT - 1, -1)),
    )
    x = jnp.where(lane < MAIN, 1 + high(lane), jnp.where(tail, tail_x, side))
    y = jnp.where(
        lane < MAIN,
        1 + low(lane),
        jnp.where(tail, jnp.where(second, EXTENT - 1, 0), 1 + low(r)),
    )
    return x, y


def mode_index(lane):
    r, tail, second, along = rest_of(lane)
    a = jnp.where(lane < MAIN, high(lane), jnp.where(tail, along, SPAN + high(r)))
    b = jnp.where(
        lane < MAIN,
        low(lane),
        jnp.where(tail, jnp.where(second, SPAN + 1, SPAN), low(r)),
    )
    return a, b


def store_split(ref, table):
    hi, lo = split(table)
    rows = table.shape[0]
    ref[:, 0:MAIN] = hi[:, :MAIN]
    ref[:, MAIN : 2 * MAIN] = hi[:, :MAIN]
    ref[:, 2 * MAIN : 3 * MAIN] = lo[:, :MAIN]
    lane = iota((rows, MAIN), 1)
    wide = table[:, MAIN:]
    top = wide.astype(BF16).astype(F32)
    mixed = jnp.where(lane < 2 * REST, top, wide - top)
    ref[:, 3 * MAIN :] = jnp.where(lane < 3 * REST, mixed, 0.0).astype(BF16)


def kernel(
    groups,
    members,
    direct,
    res_hbm,
    hvec_hbm,
    hval_hbm,
    ztab_hbm,
    zval_hbm,
    agg_hbm,
    inv_hbm,
    out_hbm,
    res,
    hvec,
    hval,
    ztab,
    zval,
    agg,
    inv,
    out,
    hpad,
    apad,
    ysend,
    csend,
    xrecv,
    yrecv,
    crecv,
    msg,
    box,
    fwd,
    bwd,
    recip,
    zfwd,
    zbwd,
    part,
    in_sem,
    out_sem,
    halo_send,
    halo_recv,
    all_send,
    all_recv,
):
    vectors, _, span_y, span_z = res.shape
    count_y = span_y // SPAN
    count_z = span_z // SPAN
    modes_z = count_z * EXTENT
    total = groups * members
    g = lax.axis_index("group")
    m = lax.axis_index("member")
    me = g * members + m

    def wrap(i, n):
        return jnp.where(i >= n, i - n, i)

    def shifted(dx, dy):
        return (wrap(g + dx % groups, groups), wrap(m + dy % members, members))

    plane = groups // PLANES
    first = g // plane * plane
    inside = g - first

    def near_peers():
        peers = [(g, wrap(m + dy, members)) for dy in range(1, members)]
        for dx in range(1, plane):
            other = first + wrap(inside + dx, plane)
            peers += [(other, wrap(m + dy, members)) for dy in range(members)]
        return peers

    def far_peers():
        return [(wrap(g + plane * dz, groups), m) for dz in range(1, PLANES)]

    near_total = plane * members

    barrier = pltpu.get_barrier_semaphore()
    loads = [
        pltpu.make_async_copy(src, dst, in_sem.at[i])
        for i, (src, dst) in enumerate(
            [
                (res_hbm, res),
                (agg_hbm, agg),
                (inv_hbm, inv),
                (hvec_hbm, hvec),
                (hval_hbm, hval),
                (ztab_hbm, ztab),
                (zval_hbm, zval),
            ]
        )
    ]
    for load in loads:
        load.start()
    corner_dy = (1,) if members == 2 else (1, -1)
    around = [(1, 0), (-1, 0), (0, 1)] + [(0, -1)] * (members > 2)
    around += [(dx, dy) for dx in (1, -1) for dy in corner_dy]
    partners = [shifted(dx, dy) for dx, dy in around]
    if direct:
        partners += near_peers() + far_peers()
    for device in partners:
        pl.semaphore_signal(barrier, inc=1, device_id=device, device_id_type=MESH)
    hpad[...] = jnp.zeros_like(hpad)
    apad[...] = jnp.zeros_like(apad)

    wide = 2 * MAIN
    lane = iota((1, wide), 1)
    row = iota((TAIL, wide), 0)
    eye = hot(iota((TAIL, 128), 0) == iota((TAIL, 128), 1))
    px, py = point_index(lane)
    ma, mb = mode_index(lane)
    px, py, ma, mb = [hot(i == row) for i in (px, py, ma, mb)]
    stacked = count_z * EXTENT
    mode = iota((1, modes_z), 1)
    mode_layer = mode // EXTENT
    mode_inner = mode - EXTENT * mode_layer
    tiled = hot(mode_inner == iota((EXTENT, modes_z), 0))
    zz = iota((span_z, stacked), 0)
    layer = iota((1, stacked), 1) % count_z
    inner = iota((1, stacked), 1) // count_z
    band = hot(zz == SPAN * layer - 1 + inner)
    near = hot((high(zz) == layer) & (inner == low(zz) + 1))
    eye_z = hot(iota((modes_z, modes_z), 0) == iota((modes_z, modes_z), 1))
    row8 = iota((8, span_z), 0)
    spread = hot(high(iota((count_z, span_z), 1)) == iota((count_z, span_z), 0))
    for load in loads[1:]:
        load.wait()

    hpad[0, 0:EXTENT, 0:EXTENT] = hvec[:, 0, :]
    hpad[1, 0:EXTENT, 0:EXTENT] = hvec[:, 1, :]
    xe = choose(turn(eye, hpad[0]), px)
    ye = choose(turn(eye, hpad[1]), py)
    body = xe[:EXTENT][:, None, :] * ye[:SPAN][None, :, :]
    table = jnp.concatenate(
        [
            body.reshape(EXTENT * SPAN, wide),
            xe * ye[SPAN : SPAN + 1, :],
            xe * ye[SPAN + 1 : SPAN + 2, :],
        ],
        axis=0,
    )
    store_split(fwd, table)
    xb = choose(hpad[0, 1 : SPAN + 1, 0:TAIL], ma)
    yb = choose(hpad[1, 1 : SPAN + 1, 0:TAIL], mb)
    store_split(bwd, (xb[:, None, :] * yb[None, :, :]).reshape(MAIN, wide))

    if direct:
        half = inv.shape[1]
        labels = dot(agg[0].astype(F32), spread.astype(F32))
        row_id = iota((2 * half, span_z), 0).astype(F32)
        member_of = jnp.concatenate(
            [hot(labels[j : j + 1, :] == row_id) for j in range(count_y)], axis=1
        )
        apad[:, 0:half] = inv[...]
    loads[0].wait()

    for v in range(vectors):
        ysend[0, v] = res[v, :, span_y - 1, :]
        ysend[1, v] = res[v, :, 0, :]
    for cx in range(2):
        for cy in range(2):
            for v in range(vectors):
                row = cx * 4 + cy * 2 + v
                y_at = (span_y - 1) * cy
                csend[row : row + 1, :] = res[v, (SPAN - 1) * cx, y_at : y_at + 1, :]

    if direct:
        sums = []
        for j in range(count_y):
            placed = jnp.zeros((8, span_z), F32)
            for v in range(vectors):
                tot = jnp.sum(res[v, :, j * SPAN : (j + 1) * SPAN, :], axis=0)
                tot = jnp.sum(tot, axis=0, keepdims=True)
                placed = placed + jnp.where((row8 & 3) == v, tot, 0.0)
            sums.append(placed)
        hi, lo = split(jnp.concatenate(sums, axis=1))
        rhs = WEIGHT * (bdot_t(hi, member_of) + bdot_t(lo, member_of))
        lane8 = iota((8, 2 * half), 1)
        rhs = jnp.where(row8 < 4, pltpu.roll(rhs, half, 1), rhs)
        mine = apad[...] + jnp.where(lane8 < half, 0.0, rhs)
        msg[me] = mine
        box[...] = mine

    halo = []

    def send(src, dst, dx, dy):
        i = len(halo)
        copy = pltpu.make_async_remote_copy(
            src_ref=src,
            dst_ref=dst,
            send_sem=halo_send.at[i],
            recv_sem=halo_recv.at[i],
            device_id=shifted(dx, dy),
            device_id_type=MESH,
        )
        halo.append(copy)

    send(res.at[:, SPAN - 1], xrecv.at[0], 1, 0)
    send(res.at[:, 0], xrecv.at[1], -1, 0)
    for ix, dx in enumerate((1, -1)):
        for iy, dy in enumerate(corner_dy):
            send(csend, crecv.at[ix, iy], dx, dy)
    send(ysend.at[0], yrecv.at[0], 0, 1)
    send(ysend.at[1], yrecv.at[1], 0, -1)

    pl.semaphore_wait(barrier, len(partners))
    for copy in halo:
        copy.start()
    if direct:
        near_copies = [
            pltpu.make_async_remote_copy(
                src_ref=box,
                dst_ref=msg.at[me],
                send_sem=all_send.at[i],
                recv_sem=all_recv.at[i],
                device_id=device,
                device_id_type=MESH,
            )
            for i, device in enumerate(near_peers())
        ]
        for copy in near_copies:
            copy.start()

    diag = choose(ztab[...].reshape(stacked, EXTENT), tiled)
    diag = jnp.where(mode_layer == iota((stacked, modes_z), 0) % count_z, diag, 0.0)
    hi, lo = split(place(band, diag))
    zfwd[0:span_z, :] = hi
    zfwd[span_z : 2 * span_z, :] = lo
    zfwd[2 * span_z : 3 * span_z, :] = hi
    hi, lo = split(turn(eye_z, place(near, diag)))
    zbwd[:, 0:span_z] = hi
    zbwd[:, span_z : 2 * span_z] = lo

    lane_h = iota((ROWS, EXTENT), 1)
    row_h = iota((ROWS, EXTENT), 0)
    t = row_h - EXTENT * SPAN
    along = jnp.where(t >= TAIL, t - TAIL, t)
    a_of = jnp.where(t < 0, high(row_h), along)
    b_of = jnp.where(t < 0, low(row_h), jnp.where(t >= TAIL, SPAN + 1, SPAN))
    column = jnp.where(lane_h == a_of, hval[0:1, :], 0.0)
    column = column + jnp.where(lane_h == b_of, hval[1:2, :], 0.0)
    column = jnp.sum(column, axis=1, keepdims=True)
    levels = dot(zval[...], tiled.astype(F32))
    level_own = mode_layer == iota((count_z, modes_z), 0)
    levels = jnp.sum(jnp.where(level_own, levels, 0.0), axis=0, keepdims=True)
    recip[...] = 1.0 / (column + levels)

    for v in range(vectors):
        field = jnp.concatenate(
            [
                res[v, :, j * SPAN : (j + 1) * SPAN, :].reshape(MAIN, span_z)
                for j in range(count_y)
            ],
            axis=1,
        )
        hi, lo = split(field)
        part[v] = bdot(fwd[:, 0 : 3 * MAIN], jnp.concatenate([hi, lo, hi], axis=0))

    if direct:
        for copy in near_copies:
            copy.wait_recv()
        slab = pl.ds(first * members, near_total)
        far_copies = [
            pltpu.make_async_remote_copy(
                src_ref=msg.at[slab],
                dst_ref=msg.at[slab],
                send_sem=all_send.at[near_total - 1 + i],
                recv_sem=all_recv.at[near_total - 1 + i],
                device_id=device,
                device_id_type=MESH,
            )
            for i, device in enumerate(far_peers())
        ]
        for copy in far_copies:
            copy.start()
    for copy in halo:
        copy.wait_recv()

    rim_row = iota((8, span_z), 0)
    solved = []
    for v in range(vectors):
        rests = []
        for j in range(count_y):
            rows = slice(j * SPAN, (j + 1) * SPAN)
            pieces = [xrecv[0, v, rows, :], xrecv[1, v, rows, :]]
            for side in range(2):
                at = j * SPAN - 1 if side == 0 else (j + 1) * SPAN
                if 0 <= at < span_y:
                    pieces.append(res[v, :, at, :])
                    before = xrecv[0, v, at : at + 1, :]
                    after = xrecv[1, v, at : at + 1, :]
                else:
                    pieces.append(yrecv[side, v])
                    iy = 0 if members == 2 else side
                    cy = 1 - side
                    r0, r1 = 4 + cy * 2 + v, cy * 2 + v
                    before = crecv[0, iy, r0 : r0 + 1, :]
                    after = crecv[1, iy, r1 : r1 + 1, :]
                pieces.append(
                    jnp.where(rim_row == 0, before, jnp.where(rim_row == 1, after, 0.0))
                )
            rests.append(jnp.concatenate(pieces, axis=0))
        hi, lo = split(jnp.concatenate(rests, axis=1))
        hat = part[v] + bdot(fwd[:, 3 * MAIN :][:, : 3 * REST], jnp.concatenate([hi, lo, hi], axis=0))
        backs = []
        for j in range(count_y):
            hi, lo = split(hat[:, j * span_z : (j + 1) * span_z])
            spectral = bdot(jnp.concatenate([hi, hi, lo], axis=1), zfwd[...]) * recip[...]
            hi, lo = split(spectral)
            both = bdot(hi, zbwd[...])
            backs.append(
                both[:, :span_z] + both[:, span_z:] + bdot(lo, zbwd[:, 0:span_z])
            )
        solved.append(jnp.concatenate(backs, axis=1))

    updates = None
    if direct:
        for copy in far_copies:
            copy.wait_recv()
        blocks = msg[...]
        whole = pltpu.roll(jnp.sum(blocks, axis=0), half, 1)
        whole = jnp.where(lane8 < half, whole, 0.0)
        blocks = blocks.reshape(groups, members, 8, 2 * half)
        answer = jnp.zeros((8, groups * 8), F32)
        for part_m in range(members):
            chosen = jnp.where(row8 // 4 == part_m, whole, 0.0)
            answer = answer + dot_t(chosen, blocks[:, part_m].reshape(groups * 8, 2 * half))
        updates = WEIGHT * choose(answer, member_of)

    stores = []
    for v in range(vectors):
        hi, lo = split(solved[v])
        result = bdot(
            bwd[:, 0 : 3 * MAIN],
            jnp.concatenate([hi[:MAIN], lo[:MAIN], hi[:MAIN]], axis=0),
        ) + bdot(
            bwd[:, 3 * MAIN :][:, : 3 * REST],
            jnp.concatenate([hi[MAIN:], lo[MAIN:], hi[MAIN:]], axis=0),
        )
        for j in range(count_y):
            piece = result[:, j * span_z : (j + 1) * span_z]
            if direct:
                lanes = slice(j * span_z, (j + 1) * span_z)
                piece = piece + (updates[v : v + 1, lanes] + updates[4 + v : 5 + v, lanes])
            out[v, :, j * SPAN : (j + 1) * SPAN, :] = piece.reshape(SPAN, SPAN, span_z)
        store = pltpu.make_async_copy(out.at[v], out_hbm.at[v], out_sem.at[v])
        store.start()
        stores.append(store)

    for copy in halo:
        copy.wait_send()
    if direct:
        for copy in near_copies + far_copies:
            copy.wait_send()
    for store in stores:
        store.wait()


def on_device(
    residual,
    horiz_vectors,
    horiz_values,
    upward_eigen_tables,
    upward_eigen_values,
    aggregate_map,
    coarse_inverse,
):
    groups = lax.axis_size("group")
    members = lax.axis_size("member")
    vectors, points_x, span_y, span_z = residual.shape
    count_y = span_y // SPAN
    count_z = span_z // SPAN
    total = groups * members
    rows, cols = coarse_inverse.shape
    direct = total <= 64 and members == 2 and rows == 8 and cols == 64 and groups * 8 == 128
    direct = direct and groups % PLANES == 0
    operands = (
        residual,
        jnp.transpose(horiz_vectors, (1, 0, 2)),
        horiz_values,
        jnp.transpose(upward_eigen_tables, (1, 0, 2)),
        upward_eigen_values,
        aggregate_map,
        coarse_inverse,
    )
    corners = 1 if members == 2 else 2
    halos = 4 + 2 * corners
    dma = pltpu.SemaphoreType.DMA
    scratch = [pltpu.VMEM(a.shape, a.dtype) for a in operands]
    scratch += [
        pltpu.VMEM(residual.shape, F32),
        pltpu.VMEM((2, TAIL, 128), F32),
        pltpu.VMEM((8, 128), F32),
        pltpu.VMEM((2, vectors, SPAN, span_z), F32),
        pltpu.VMEM((8, span_z), F32),
        pltpu.VMEM((2, vectors, span_y, span_z), F32),
        pltpu.VMEM((2, vectors, SPAN, span_z), F32),
        pltpu.VMEM((2, corners, 8, span_z), F32),
        pltpu.VMEM((total if direct else 1, 8, 128), F32),
        pltpu.VMEM((8, 128), F32),
        pltpu.VMEM((ROWS, 4 * MAIN), BF16),
        pltpu.VMEM((MAIN, 4 * MAIN), BF16),
        pltpu.VMEM((ROWS, count_z * EXTENT), F32),
        pltpu.VMEM((3 * span_z, count_z * EXTENT), BF16),
        pltpu.VMEM((count_z * EXTENT, 2 * span_z), BF16),
        pltpu.VMEM((vectors, ROWS, count_y * span_z), F32),
        dma((len(operands),)),
        dma((vectors,)),
        dma((halos,)),
        dma((halos,)),
        dma((groups // PLANES * members + PLANES,)),
        dma((groups // PLANES * members + PLANES,)),
    ]
    result = pl.pallas_call(
        functools.partial(kernel, groups, members, direct),
        out_shape=jax.ShapeDtypeStruct(residual.shape, F32),
        in_specs=[pl.BlockSpec(memory_space=pltpu.HBM)] * len(operands),
        out_specs=pl.BlockSpec(memory_space=pl.ANY),
        scratch_shapes=scratch,
        compiler_params=pltpu.CompilerParams(
            collective_id=0, has_side_effects=True, vmem_limit_bytes=60 * 1024 * 1024
        ),
        cost_estimate=pl.CostEstimate(
            flops=2 * 10**9, bytes_accessed=2**20, transcendentals=0
        ),
    )(*operands)
    if direct:
        return result
    totals = residual.reshape(vectors, SPAN, count_y, SPAN, count_z, SPAN).sum(axis=(1, 3, 5))
    labels = aggregate_map.reshape(-1)
    partial_rhs = WEIGHT * jax.ops.segment_sum(
        totals.reshape(vectors, -1).T, labels, num_segments=rows * groups
    ).T
    whole_rhs = lax.psum(partial_rhs, ("group", "member"))
    share = lax.dynamic_slice_in_dim(whole_rhs, lax.axis_index("member") * cols, cols, 1)
    row_values = lax.psum(dot(share, coarse_inverse.T), "member")
    coarse = lax.all_gather(row_values, "group", axis=1, tiled=True)
    update = WEIGHT * jnp.take(coarse, labels, axis=1)
    update = update.reshape(vectors, 1, count_y, 1, count_z, 1)
    split_up = (vectors, SPAN, count_y, SPAN, count_z, SPAN)
    return (result.reshape(split_up) + update).reshape(residual.shape)


def solution(mesh):
    in_specs = (
        P(None, "group", "member", None),
        P(),
        P(),
        P(),
        P(),
        P("group", "member", None),
        P("group", "member"),
    )
    out_specs = P(None, "group", "member", None)
    return jax.shard_map(
        on_device, mesh=mesh, in_specs=in_specs, out_specs=out_specs, check_vma=False
    )
```

```python
import functools

import jax
import jax.numpy as jnp
from jax import lax
from jax.experimental import pallas as pl
from jax.experimental.pallas import tpu as pltpu
from jax.sharding import PartitionSpec as P

SPAN = 16
EXTENT = SPAN + 2
MAIN = SPAN * SPAN
TAIL = 24
REST = 2 * SPAN + 2 * TAIL
ROWS = MAIN + REST
WEIGHT = float(SPAN) ** (-1.5)
MESH = pl.DeviceIdType.MESH
F32 = jnp.float32
BF16 = jnp.bfloat16


def iota(shape, dim):
    return lax.broadcasted_iota(jnp.int32, shape, dim)


def dot(a, b):
    return jnp.dot(a, b, precision=lax.Precision.HIGHEST, preferred_element_type=F32)


def dot_t(a, b):
    dims = (((1,), (1,)), ((), ()))
    return lax.dot_general(
        a, b, dims, precision=lax.Precision.HIGHEST, preferred_element_type=F32
    )


def bdot(a, b):
    return jnp.dot(a, b, preferred_element_type=F32)


def bdot_t(a, b):
    dims = (((1,), (1,)), ((), ()))
    return lax.dot_general(a, b, dims, preferred_element_type=F32)


def split(a):
    hi = a.astype(BF16)
    return hi, (a - hi.astype(F32)).astype(BF16)


def choose(a, hot):
    hi, lo = split(a)
    return bdot(hi, hot) + bdot(lo, hot)


def place(hot, a):
    hi, lo = split(a)
    return bdot(hot, hi) + bdot(hot, lo)


def turn(hot, a):
    hi, lo = split(a)
    return bdot_t(hot, hi) + bdot_t(hot, lo)


def hot(condition):
    return condition.astype(F32).astype(BF16)


def high(i):
    return lax.shift_right_logical(i, 4)


def low(i):
    return i & (SPAN - 1)


def rest_of(lane):
    r = lane - MAIN
    r = jnp.where(r >= 2 * REST, r - 2 * REST, jnp.where(r >= REST, r - REST, r))
    t = r - 2 * SPAN
    tail = (t >= 0) & (lane < MAIN + 3 * REST)
    second = t >= TAIL
    return r, tail, second, jnp.where(second, t - TAIL, t)


def point_index(lane):
    r, tail, second, along = rest_of(lane)
    side = jnp.where(r >= SPAN, EXTENT - 1, 0)
    tail_x = jnp.where(
        along < SPAN,
        along + 1,
        jnp.where(along == SPAN, 0, jnp.where(along == SPAN + 1, EXTENT - 1, -1)),
    )
    x = jnp.where(lane < MAIN, 1 + high(lane), jnp.where(tail, tail_x, side))
    y = jnp.where(
        lane < MAIN,
        1 + low(lane),
        jnp.where(tail, jnp.where(second, EXTENT - 1, 0), 1 + low(r)),
    )
    return x, y


def mode_index(lane):
    r, tail, second, along = rest_of(lane)
    a = jnp.where(lane < MAIN, high(lane), jnp.where(tail, along, SPAN + high(r)))
    b = jnp.where(
        lane < MAIN,
        low(lane),
        jnp.where(tail, jnp.where(second, SPAN + 1, SPAN), low(r)),
    )
    return a, b


def store_split(ref, table):
    hi, lo = split(table)
    rows = table.shape[0]
    ref[:, 0:MAIN] = hi[:, :MAIN]
    ref[:, MAIN : 2 * MAIN] = hi[:, :MAIN]
    ref[:, 2 * MAIN : 3 * MAIN] = lo[:, :MAIN]
    lane = iota((rows, MAIN), 1)
    wide = table[:, MAIN:]
    top = wide.astype(BF16).astype(F32)
    mixed = jnp.where(lane < 2 * REST, top, wide - top)
    ref[:, 3 * MAIN :] = jnp.where(lane < 3 * REST, mixed, 0.0).astype(BF16)


def kernel(
    groups,
    members,
    direct,
    res_hbm,
    hvec_hbm,
    hval_hbm,
    ztab_hbm,
    zval_hbm,
    agg_hbm,
    inv_hbm,
    out_hbm,
    res,
    hvec,
    hval,
    ztab,
    zval,
    agg,
    inv,
    out,
    hpad,
    apad,
    ysend,
    csend,
    xrecv,
    yrecv,
    crecv,
    msg,
    box,
    fwd,
    bwd,
    recip,
    zfwd,
    zbwd,
    part,
    in_sem,
    out_sem,
    halo_send,
    halo_recv,
    all_send,
    all_recv,
):
    vectors, _, span_y, span_z = res.shape
    count_y = span_y // SPAN
    count_z = span_z // SPAN
    modes_z = count_z * EXTENT
    total = groups * members
    g = lax.axis_index("group")
    m = lax.axis_index("member")
    me = g * members + m

    def wrap(i, n):
        return jnp.where(i >= n, i - n, i)

    def shifted(dx, dy):
        return (wrap(g + dx % groups, groups), wrap(m + dy % members, members))

    def peers():
        found = [(g, wrap(m + dy, members)) for dy in range(1, members)]
        for dx in range(1, groups):
            other = wrap(g + dx, groups)
            found += [(other, wrap(m + dy, members)) for dy in range(members)]
        return found

    barrier = pltpu.get_barrier_semaphore()
    loads = [
        pltpu.make_async_copy(src, dst, in_sem.at[i])
        for i, (src, dst) in enumerate(
            [
                (res_hbm, res),
                (agg_hbm, agg),
                (inv_hbm, inv),
                (hvec_hbm, hvec),
                (hval_hbm, hval),
                (ztab_hbm, ztab),
                (zval_hbm, zval),
            ]
        )
    ]
    for load in loads:
        load.start()
    corner_dy = (1,) if members == 2 else (1, -1)
    around = [(1, 0), (-1, 0), (0, 1)] + [(0, -1)] * (members > 2)
    around += [(dx, dy) for dx in (1, -1) for dy in corner_dy]
    partners = peers() if direct else [shifted(dx, dy) for dx, dy in around]
    for device in partners:
        pl.semaphore_signal(barrier, inc=1, device_id=device, device_id_type=MESH)
    hpad[...] = jnp.zeros_like(hpad)
    apad[...] = jnp.zeros_like(apad)

    wide = 2 * MAIN
    lane = iota((1, wide), 1)
    row = iota((TAIL, wide), 0)
    eye = hot(iota((TAIL, 128), 0) == iota((TAIL, 128), 1))
    px, py = point_index(lane)
    ma, mb = mode_index(lane)
    px, py, ma, mb = [hot(i == row) for i in (px, py, ma, mb)]
    stacked = count_z * EXTENT
    mode = iota((1, modes_z), 1)
    mode_layer = mode // EXTENT
    mode_inner = mode - EXTENT * mode_layer
    tiled = hot(mode_inner == iota((EXTENT, modes_z), 0))
    zz = iota((span_z, stacked), 0)
    layer = iota((1, stacked), 1) % count_z
    inner = iota((1, stacked), 1) // count_z
    band = hot(zz == SPAN * layer - 1 + inner)
    near = hot((high(zz) == layer) & (inner == low(zz) + 1))
    eye_z = hot(iota((modes_z, modes_z), 0) == iota((modes_z, modes_z), 1))
    row8 = iota((8, span_z), 0)
    spread = hot(high(iota((count_z, span_z), 1)) == iota((count_z, span_z), 0))
    for load in loads[1:]:
        load.wait()

    if direct:
        half = inv.shape[1]
        labels = dot(agg[0].astype(F32), spread.astype(F32))
        row_id = iota((2 * half, span_z), 0).astype(F32)
        member_of = jnp.concatenate(
            [hot(labels[j : j + 1, :] == row_id) for j in range(count_y)], axis=1
        )
        apad[:, 0:half] = inv[...]
    loads[0].wait()

    for v in range(vectors):
        ysend[0, v] = res[v, :, span_y - 1, :]
        ysend[1, v] = res[v, :, 0, :]
    for cx in range(2):
        for cy in range(2):
            for v in range(vectors):
                row = cx * 4 + cy * 2 + v
                y_at = (span_y - 1) * cy
                csend[row : row + 1, :] = res[v, (SPAN - 1) * cx, y_at : y_at + 1, :]

    if direct:
        sums = []
        for j in range(count_y):
            placed = jnp.zeros((8, span_z), F32)
            for v in range(vectors):
                tot = jnp.sum(res[v, :, j * SPAN : (j + 1) * SPAN, :], axis=0)
                tot = jnp.sum(tot, axis=0, keepdims=True)
                placed = placed + jnp.where((row8 & 3) == v, tot, 0.0)
            sums.append(placed)
        hi, lo = split(jnp.concatenate(sums, axis=1))
        rhs = WEIGHT * (bdot_t(hi, member_of) + bdot_t(lo, member_of))
        lane8 = iota((8, 2 * half), 1)
        rhs = jnp.where(row8 < 4, pltpu.roll(rhs, half, 1), rhs)
        mine = apad[...] + jnp.where(lane8 < half, 0.0, rhs)
        msg[me] = mine
        box[...] = mine

    halo = []

    def send(src, dst, dx, dy):
        i = len(halo)
        copy = pltpu.make_async_remote_copy(
            src_ref=src,
            dst_ref=dst,
            send_sem=halo_send.at[i],
            recv_sem=halo_recv.at[i],
            device_id=shifted(dx, dy),
            device_id_type=MESH,
        )
        halo.append(copy)

    send(res.at[:, SPAN - 1], xrecv.at[0], 1, 0)
    send(res.at[:, 0], xrecv.at[1], -1, 0)
    for ix, dx in enumerate((1, -1)):
        for iy, dy in enumerate(corner_dy):
            send(csend, crecv.at[ix, iy], dx, dy)
    send(ysend.at[0], yrecv.at[0], 0, 1)
    send(ysend.at[1], yrecv.at[1], 0, -1)

    pl.semaphore_wait(barrier, len(partners))
    for copy in halo:
        copy.start()
    if direct:
        shares = [
            pltpu.make_async_remote_copy(
                src_ref=box,
                dst_ref=msg.at[me],
                send_sem=all_send,
                recv_sem=all_recv,
                device_id=device,
                device_id_type=MESH,
            )
            for device in partners
        ]
        for copy in shares:
            copy.start()

    hpad[0, 0:EXTENT, 0:EXTENT] = hvec[:, 0, :]
    hpad[1, 0:EXTENT, 0:EXTENT] = hvec[:, 1, :]
    xe = choose(turn(eye, hpad[0]), px)
    ye = choose(turn(eye, hpad[1]), py)
    body = xe[:EXTENT][:, None, :] * ye[:SPAN][None, :, :]
    table = jnp.concatenate(
        [
            body.reshape(EXTENT * SPAN, wide),
            xe * ye[SPAN : SPAN + 1, :],
            xe * ye[SPAN + 1 : SPAN + 2, :],
        ],
        axis=0,
    )
    store_split(fwd, table)
    xb = choose(hpad[0, 1 : SPAN + 1, 0:TAIL], ma)
    yb = choose(hpad[1, 1 : SPAN + 1, 0:TAIL], mb)
    store_split(bwd, (xb[:, None, :] * yb[None, :, :]).reshape(MAIN, wide))

    diag = choose(ztab[...].reshape(stacked, EXTENT), tiled)
    diag = jnp.where(mode_layer == iota((stacked, modes_z), 0) % count_z, diag, 0.0)
    hi, lo = split(place(band, diag))
    zfwd[0:span_z, :] = hi
    zfwd[span_z : 2 * span_z, :] = lo
    zfwd[2 * span_z : 3 * span_z, :] = hi
    hi, lo = split(turn(eye_z, place(near, diag)))
    zbwd[:, 0:span_z] = hi
    zbwd[:, span_z : 2 * span_z] = lo

    lane_h = iota((ROWS, EXTENT), 1)
    row_h = iota((ROWS, EXTENT), 0)
    t = row_h - EXTENT * SPAN
    along = jnp.where(t >= TAIL, t - TAIL, t)
    a_of = jnp.where(t < 0, high(row_h), along)
    b_of = jnp.where(t < 0, low(row_h), jnp.where(t >= TAIL, SPAN + 1, SPAN))
    column = jnp.where(lane_h == a_of, hval[0:1, :], 0.0)
    column = column + jnp.where(lane_h == b_of, hval[1:2, :], 0.0)
    column = jnp.sum(column, axis=1, keepdims=True)
    levels = dot(zval[...], tiled.astype(F32))
    level_own = mode_layer == iota((count_z, modes_z), 0)
    levels = jnp.sum(jnp.where(level_own, levels, 0.0), axis=0, keepdims=True)
    recip[...] = 1.0 / (column + levels)

    for v in range(vectors):
        field = jnp.concatenate(
            [
                res[v, :, j * SPAN : (j + 1) * SPAN, :].reshape(MAIN, span_z)
                for j in range(count_y)
            ],
            axis=1,
        )
        hi, lo = split(field)
        part[v] = bdot(fwd[:, 0 : 3 * MAIN], jnp.concatenate([hi, lo, hi], axis=0))

    for copy in halo:
        copy.wait_recv()

    rim_row = iota((8, span_z), 0)
    solved = []
    for v in range(vectors):
        rests = []
        for j in range(count_y):
            rows = slice(j * SPAN, (j + 1) * SPAN)
            pieces = [xrecv[0, v, rows, :], xrecv[1, v, rows, :]]
            for side in range(2):
                at = j * SPAN - 1 if side == 0 else (j + 1) * SPAN
                if 0 <= at < span_y:
                    pieces.append(res[v, :, at, :])
                    before = xrecv[0, v, at : at + 1, :]
                    after = xrecv[1, v, at : at + 1, :]
                else:
                    pieces.append(yrecv[side, v])
                    iy = 0 if members == 2 else side
                    cy = 1 - side
                    r0, r1 = 4 + cy * 2 + v, cy * 2 + v
                    before = crecv[0, iy, r0 : r0 + 1, :]
                    after = crecv[1, iy, r1 : r1 + 1, :]
                pieces.append(
                    jnp.where(rim_row == 0, before, jnp.where(rim_row == 1, after, 0.0))
                )
            rests.append(jnp.concatenate(pieces, axis=0))
        hi, lo = split(jnp.concatenate(rests, axis=1))
        hat = part[v] + bdot(fwd[:, 3 * MAIN :][:, : 3 * REST], jnp.concatenate([hi, lo, hi], axis=0))
        backs = []
        for j in range(count_y):
            hi, lo = split(hat[:, j * span_z : (j + 1) * span_z])
            spectral = bdot(jnp.concatenate([hi, hi, lo], axis=1), zfwd[...]) * recip[...]
            hi, lo = split(spectral)
            both = bdot(hi, zbwd[...])
            backs.append(
                both[:, :span_z] + both[:, span_z:] + bdot(lo, zbwd[:, 0:span_z])
            )
        solved.append(jnp.concatenate(backs, axis=1))

    updates = None
    if direct:
        everyone = msg.at[pl.ds(0, total - 1)]
        pltpu.make_async_copy(everyone, everyone, all_recv).wait()
        blocks = msg[...]
        whole = pltpu.roll(jnp.sum(blocks, axis=0), half, 1)
        whole = jnp.where(lane8 < half, whole, 0.0)
        blocks = blocks.reshape(groups, members, 8, 2 * half)
        answer = jnp.zeros((8, groups * 8), F32)
        for part_m in range(members):
            chosen = jnp.where(row8 // 4 == part_m, whole, 0.0)
            answer = answer + dot_t(chosen, blocks[:, part_m].reshape(groups * 8, 2 * half))
        updates = WEIGHT * choose(answer, member_of)

    stores = []
    for v in range(vectors):
        hi, lo = split(solved[v])
        result = bdot(
            bwd[:, 0 : 3 * MAIN],
            jnp.concatenate([hi[:MAIN], lo[:MAIN], hi[:MAIN]], axis=0),
        ) + bdot(
            bwd[:, 3 * MAIN :][:, : 3 * REST],
            jnp.concatenate([hi[MAIN:], lo[MAIN:], hi[MAIN:]], axis=0),
        )
        for j in range(count_y):
            piece = result[:, j * span_z : (j + 1) * span_z]
            if direct:
                lanes = slice(j * span_z, (j + 1) * span_z)
                piece = piece + (updates[v : v + 1, lanes] + updates[4 + v : 5 + v, lanes])
            out[v, :, j * SPAN : (j + 1) * SPAN, :] = piece.reshape(SPAN, SPAN, span_z)
        store = pltpu.make_async_copy(out.at[v], out_hbm.at[v], out_sem.at[v])
        store.start()
        stores.append(store)

    for copy in halo:
        copy.wait_send()
    if direct:
        pltpu.make_async_copy(everyone, everyone, all_send).wait()
    for store in stores:
        store.wait()


def on_device(
    residual,
    horiz_vectors,
    horiz_values,
    upward_eigen_tables,
    upward_eigen_values,
    aggregate_map,
    coarse_inverse,
):
    groups = lax.axis_size("group")
    members = lax.axis_size("member")
    vectors, points_x, span_y, span_z = residual.shape
    count_y = span_y // SPAN
    count_z = span_z // SPAN
    total = groups * members
    rows, cols = coarse_inverse.shape
    direct = total <= 64 and members == 2 and rows == 8 and cols == 64 and groups * 8 == 128
    operands = (
        residual,
        jnp.transpose(horiz_vectors, (1, 0, 2)),
        horiz_values,
        jnp.transpose(upward_eigen_tables, (1, 0, 2)),
        upward_eigen_values,
        aggregate_map,
        coarse_inverse,
    )
    corners = 1 if members == 2 else 2
    halos = 4 + 2 * corners
    dma = pltpu.SemaphoreType.DMA
    scratch = [pltpu.VMEM(a.shape, a.dtype) for a in operands]
    scratch += [
        pltpu.VMEM(residual.shape, F32),
        pltpu.VMEM((2, TAIL, 128), F32),
        pltpu.VMEM((8, 128), F32),
        pltpu.VMEM((2, vectors, SPAN, span_z), F32),
        pltpu.VMEM((8, span_z), F32),
        pltpu.VMEM((2, vectors, span_y, span_z), F32),
        pltpu.VMEM((2, vectors, SPAN, span_z), F32),
        pltpu.VMEM((2, corners, 8, span_z), F32),
        pltpu.VMEM((total if direct else 1, 8, 128), F32),
        pltpu.VMEM((8, 128), F32),
        pltpu.VMEM((ROWS, 4 * MAIN), BF16),
        pltpu.VMEM((MAIN, 4 * MAIN), BF16),
        pltpu.VMEM((ROWS, count_z * EXTENT), F32),
        pltpu.VMEM((3 * span_z, count_z * EXTENT), BF16),
        pltpu.VMEM((count_z * EXTENT, 2 * span_z), BF16),
        pltpu.VMEM((vectors, ROWS, count_y * span_z), F32),
        dma((len(operands),)),
        dma((vectors,)),
        dma((halos,)),
        dma((halos,)),
        dma,
        dma,
    ]
    result = pl.pallas_call(
        functools.partial(kernel, groups, members, direct),
        out_shape=jax.ShapeDtypeStruct(residual.shape, F32),
        in_specs=[pl.BlockSpec(memory_space=pltpu.HBM)] * len(operands),
        out_specs=pl.BlockSpec(memory_space=pl.ANY),
        scratch_shapes=scratch,
        compiler_params=pltpu.CompilerParams(
            collective_id=0, has_side_effects=True, vmem_limit_bytes=60 * 1024 * 1024
        ),
        cost_estimate=pl.CostEstimate(
            flops=2 * 10**9, bytes_accessed=2**20, transcendentals=0
        ),
    )(*operands)
    if direct:
        return result
    totals = residual.reshape(vectors, SPAN, count_y, SPAN, count_z, SPAN).sum(axis=(1, 3, 5))
    labels = aggregate_map.reshape(-1)
    partial_rhs = WEIGHT * jax.ops.segment_sum(
        totals.reshape(vectors, -1).T, labels, num_segments=rows * groups
    ).T
    whole_rhs = lax.psum(partial_rhs, ("group", "member"))
    share = lax.dynamic_slice_in_dim(whole_rhs, lax.axis_index("member") * cols, cols, 1)
    row_values = lax.psum(dot(share, coarse_inverse.T), "member")
    coarse = lax.all_gather(row_values, "group", axis=1, tiled=True)
    update = WEIGHT * jnp.take(coarse, labels, axis=1)
    update = update.reshape(vectors, 1, count_y, 1, count_z, 1)
    split_up = (vectors, SPAN, count_y, SPAN, count_z, SPAN)
    return (result.reshape(split_up) + update).reshape(residual.shape)


def solution(mesh):
    in_specs = (
        P(None, "group", "member", None),
        P(),
        P(),
        P(),
        P(),
        P("group", "member", None),
        P("group", "member"),
    )
    out_specs = P(None, "group", "member", None)
    return jax.shard_map(
        on_device, mesh=mesh, in_specs=in_specs, out_specs=out_specs, check_vma=False
    )
```

```python
import functools

import jax
import jax.numpy as jnp
from jax import lax
from jax.experimental import pallas as pl
from jax.experimental.pallas import tpu as pltpu
from jax.sharding import PartitionSpec as P

SPAN = 16
EXTENT = SPAN + 2
MAIN = SPAN * SPAN
TAIL = 24
REST = 2 * SPAN + 2 * TAIL
ROWS = MAIN + REST
WEIGHT = float(SPAN) ** (-1.5)
MESH = pl.DeviceIdType.MESH
F32 = jnp.float32
BF16 = jnp.bfloat16


def iota(shape, dim):
    return lax.broadcasted_iota(jnp.int32, shape, dim)


def dot(a, b):
    return jnp.dot(a, b, precision=lax.Precision.HIGHEST, preferred_element_type=F32)


def dot_t(a, b):
    dims = (((1,), (1,)), ((), ()))
    return lax.dot_general(
        a, b, dims, precision=lax.Precision.HIGHEST, preferred_element_type=F32
    )


def bdot(a, b):
    return jnp.dot(a, b, preferred_element_type=F32)


def bdot_t(a, b):
    dims = (((1,), (1,)), ((), ()))
    return lax.dot_general(a, b, dims, preferred_element_type=F32)


def split(a):
    hi = a.astype(BF16)
    return hi, (a - hi.astype(F32)).astype(BF16)


def choose(a, hot):
    hi, lo = split(a)
    return bdot(hi, hot) + bdot(lo, hot)


def place(hot, a):
    hi, lo = split(a)
    return bdot(hot, hi) + bdot(hot, lo)


def turn(hot, a):
    hi, lo = split(a)
    return bdot_t(hot, hi) + bdot_t(hot, lo)


def hot(condition):
    return condition.astype(F32).astype(BF16)


def high(i):
    return lax.shift_right_logical(i, 4)


def low(i):
    return i & (SPAN - 1)


def rest_of(lane):
    r = lane - MAIN
    r = jnp.where(r >= 2 * REST, r - 2 * REST, jnp.where(r >= REST, r - REST, r))
    t = r - 2 * SPAN
    tail = (t >= 0) & (lane < MAIN + 3 * REST)
    second = t >= TAIL
    return r, tail, second, jnp.where(second, t - TAIL, t)


def point_index(lane):
    r, tail, second, along = rest_of(lane)
    side = jnp.where(r >= SPAN, EXTENT - 1, 0)
    tail_x = jnp.where(
        along < SPAN,
        along + 1,
        jnp.where(along == SPAN, 0, jnp.where(along == SPAN + 1, EXTENT - 1, -1)),
    )
    x = jnp.where(lane < MAIN, 1 + high(lane), jnp.where(tail, tail_x, side))
    y = jnp.where(
        lane < MAIN,
        1 + low(lane),
        jnp.where(tail, jnp.where(second, EXTENT - 1, 0), 1 + low(r)),
    )
    return x, y


def mode_index(lane):
    r, tail, second, along = rest_of(lane)
    a = jnp.where(lane < MAIN, high(lane), jnp.where(tail, along, SPAN + high(r)))
    b = jnp.where(
        lane < MAIN,
        low(lane),
        jnp.where(tail, jnp.where(second, SPAN + 1, SPAN), low(r)),
    )
    return a, b


def store_split(ref, table):
    hi, lo = split(table)
    rows = table.shape[0]
    ref[:, 0:MAIN] = hi[:, :MAIN]
    ref[:, MAIN : 2 * MAIN] = hi[:, :MAIN]
    ref[:, 2 * MAIN : 3 * MAIN] = lo[:, :MAIN]
    lane = iota((rows, MAIN), 1)
    wide = table[:, MAIN:]
    top = wide.astype(BF16).astype(F32)
    mixed = jnp.where(lane < 2 * REST, top, wide - top)
    ref[:, 3 * MAIN :] = jnp.where(lane < 3 * REST, mixed, 0.0).astype(BF16)


def kernel(
    groups,
    members,
    direct,
    res_hbm,
    hvec_hbm,
    hval_hbm,
    ztab_hbm,
    zval_hbm,
    agg_hbm,
    inv_hbm,
    out_hbm,
    res,
    hvec,
    hval,
    ztab,
    zval,
    agg,
    inv,
    out,
    hpad,
    apad,
    ysend,
    csend,
    xrecv,
    yrecv,
    crecv,
    msg,
    box,
    fwd,
    bwd,
    recip,
    zfwd,
    zbwd,
    part,
    in_sem,
    out_sem,
    halo_send,
    halo_recv,
    all_send,
    all_recv,
):
    vectors, _, span_y, span_z = res.shape
    count_y = span_y // SPAN
    count_z = span_z // SPAN
    modes_z = count_z * EXTENT
    total = groups * members
    g = lax.axis_index("group")
    m = lax.axis_index("member")
    me = g * members + m

    def wrap(i, n):
        return jnp.where(i >= n, i - n, i)

    def shifted(dx, dy):
        return (wrap(g + dx % groups, groups), wrap(m + dy % members, members))

    def peers():
        found = [(g, wrap(m + dy, members)) for dy in range(1, members)]
        for dx in range(1, groups):
            other = wrap(g + dx, groups)
            found += [(other, wrap(m + dy, members)) for dy in range(members)]
        return found

    barrier = pltpu.get_barrier_semaphore()
    loads = [
        pltpu.make_async_copy(src, dst, in_sem.at[i])
        for i, (src, dst) in enumerate(
            [
                (res_hbm, res),
                (agg_hbm, agg),
                (inv_hbm, inv),
                (hvec_hbm, hvec),
                (hval_hbm, hval),
                (ztab_hbm, ztab),
                (zval_hbm, zval),
            ]
        )
    ]
    for load in loads:
        load.start()
    corner_dy = (1,) if members == 2 else (1, -1)
    around = [(1, 0), (-1, 0), (0, 1)] + [(0, -1)] * (members > 2)
    around += [(dx, dy) for dx in (1, -1) for dy in corner_dy]
    partners = peers() if direct else [shifted(dx, dy) for dx, dy in around]
    for device in partners:
        pl.semaphore_signal(barrier, inc=1, device_id=device, device_id_type=MESH)
    hpad[...] = jnp.zeros_like(hpad)
    apad[...] = jnp.zeros_like(apad)

    wide = 2 * MAIN
    lane = iota((1, wide), 1)
    row = iota((TAIL, wide), 0)
    eye = hot(iota((TAIL, 128), 0) == iota((TAIL, 128), 1))
    px, py = point_index(lane)
    ma, mb = mode_index(lane)
    px, py, ma, mb = [hot(i == row) for i in (px, py, ma, mb)]
    stacked = count_z * EXTENT
    mode = iota((1, modes_z), 1)
    mode_layer = mode // EXTENT
    mode_inner = mode - EXTENT * mode_layer
    tiled = hot(mode_inner == iota((EXTENT, modes_z), 0))
    zz = iota((span_z, stacked), 0)
    layer = iota((1, stacked), 1) % count_z
    inner = iota((1, stacked), 1) // count_z
    band = hot(zz == SPAN * layer - 1 + inner)
    near = hot((high(zz) == layer) & (inner == low(zz) + 1))
    eye_z = hot(iota((modes_z, modes_z), 0) == iota((modes_z, modes_z), 1))
    row8 = iota((8, span_z), 0)
    spread = hot(high(iota((count_z, span_z), 1)) == iota((count_z, span_z), 0))
    for load in loads[1:]:
        load.wait()

    if direct:
        half = inv.shape[1]
        labels = dot(agg[0].astype(F32), spread.astype(F32))
        row_id = iota((2 * half, span_z), 0).astype(F32)
        member_of = [(labels[j : j + 1, :] == row_id).astype(F32) for j in range(count_y)]
        downward = hot(high(iota((span_z, count_z), 0)) == iota((span_z, count_z), 1))
        upright = dot_t(downward.astype(F32), agg[0].astype(F32))
        lane_id = iota((span_z, 2 * half), 1).astype(F32)
        owned = jnp.concatenate(
            [hot(upright[:, j : j + 1] == lane_id) for j in range(count_y)], axis=0
        )
        apad[:, 0:half] = inv[...]
    loads[0].wait()

    for v in range(vectors):
        ysend[0, v] = res[v, :, span_y - 1, :]
        ysend[1, v] = res[v, :, 0, :]
    for cx in range(2):
        for cy in range(2):
            for v in range(vectors):
                row = cx * 4 + cy * 2 + v
                y_at = (span_y - 1) * cy
                csend[row : row + 1, :] = res[v, (SPAN - 1) * cx, y_at : y_at + 1, :]

    if direct:
        sums = []
        for j in range(count_y):
            placed = jnp.zeros((8, span_z), F32)
            for v in range(vectors):
                tot = jnp.sum(res[v, :, j * SPAN : (j + 1) * SPAN, :], axis=0)
                tot = jnp.sum(tot, axis=0, keepdims=True)
                placed = placed + jnp.where((row8 & 3) == v, tot, 0.0)
            sums.append(placed)
        hi, lo = split(jnp.concatenate(sums, axis=1))
        rhs = WEIGHT * (bdot(hi, owned) + bdot(lo, owned))
        lane8 = iota((8, 2 * half), 1)
        rhs = jnp.where(row8 < 4, pltpu.roll(rhs, half, 1), rhs)
        mine = apad[...] + jnp.where(lane8 < half, 0.0, rhs)
        msg[me] = mine
        box[...] = mine

    halo = []

    def send(src, dst, dx, dy):
        i = len(halo)
        copy = pltpu.make_async_remote_copy(
            src_ref=src,
            dst_ref=dst,
            send_sem=halo_send.at[i],
            recv_sem=halo_recv.at[i],
            device_id=shifted(dx, dy),
            device_id_type=MESH,
        )
        halo.append(copy)

    send(res.at[:, SPAN - 1], xrecv.at[0], 1, 0)
    send(res.at[:, 0], xrecv.at[1], -1, 0)
    for ix, dx in enumerate((1, -1)):
        for iy, dy in enumerate(corner_dy):
            send(csend, crecv.at[ix, iy], dx, dy)
    send(ysend.at[0], yrecv.at[0], 0, 1)
    send(ysend.at[1], yrecv.at[1], 0, -1)

    pl.semaphore_wait(barrier, len(partners))
    for copy in halo:
        copy.start()
    if direct:
        shares = [
            pltpu.make_async_remote_copy(
                src_ref=box,
                dst_ref=msg.at[me],
                send_sem=all_send,
                recv_sem=all_recv,
                device_id=device,
                device_id_type=MESH,
            )
            for device in partners
        ]
        for copy in shares:
            copy.start()

    hpad[0, 0:EXTENT, 0:EXTENT] = hvec[:, 0, :]
    hpad[1, 0:EXTENT, 0:EXTENT] = hvec[:, 1, :]
    xe = choose(turn(eye, hpad[0]), px)
    ye = choose(turn(eye, hpad[1]), py)
    body = xe[:EXTENT][:, None, :] * ye[:SPAN][None, :, :]
    table = jnp.concatenate(
        [
            body.reshape(EXTENT * SPAN, wide),
            xe * ye[SPAN : SPAN + 1, :],
            xe * ye[SPAN + 1 : SPAN + 2, :],
        ],
        axis=0,
    )
    store_split(fwd, table)
    xb = choose(hpad[0, 1 : SPAN + 1, 0:TAIL], ma)
    yb = choose(hpad[1, 1 : SPAN + 1, 0:TAIL], mb)
    store_split(bwd, (xb[:, None, :] * yb[None, :, :]).reshape(MAIN, wide))

    diag = choose(ztab[...].reshape(stacked, EXTENT), tiled)
    diag = jnp.where(mode_layer == iota((stacked, modes_z), 0) % count_z, diag, 0.0)
    hi, lo = split(place(band, diag))
    zfwd[0:span_z, :] = hi
    zfwd[span_z : 2 * span_z, :] = lo
    zfwd[2 * span_z : 3 * span_z, :] = hi
    hi, lo = split(turn(eye_z, place(near, diag)))
    zbwd[:, 0:span_z] = hi
    zbwd[:, span_z : 2 * span_z] = lo

    levels = dot(zval[...], tiled.astype(F32))
    level_own = mode_layer == iota((count_z, modes_z), 0)
    levels = jnp.sum(jnp.where(level_own, levels, 0.0), axis=0, keepdims=True)
    upright_eye = (iota((TAIL, EXTENT), 0) == iota((TAIL, EXTENT), 1)).astype(F32)
    columns = dot_t(upright_eye, hval[...])
    first = jnp.broadcast_to(columns[:, 0:1], (TAIL, modes_z))
    second = columns[:, 1:2] + levels
    body = first[:EXTENT][:, None, :] + second[:SPAN][None, :, :]
    recip[0 : EXTENT * SPAN, :] = 1.0 / body.reshape(EXTENT * SPAN, modes_z)
    for side in range(2):
        rows = slice(EXTENT * SPAN + side * TAIL, EXTENT * SPAN + (side + 1) * TAIL)
        recip[rows, :] = 1.0 / (first + second[SPAN + side : SPAN + side + 1, :])

    for v in range(vectors):
        field = jnp.concatenate(
            [
                res[v, :, j * SPAN : (j + 1) * SPAN, :].reshape(MAIN, span_z)
                for j in range(count_y)
            ],
            axis=1,
        )
        hi, lo = split(field)
        part[v] = bdot(fwd[:, 0 : 3 * MAIN], jnp.concatenate([hi, lo, hi], axis=0))

    for copy in halo:
        copy.wait_recv()

    rim_row = iota((8, span_z), 0)
    solved = []
    for v in range(vectors):
        rests = []
        for j in range(count_y):
            rows = slice(j * SPAN, (j + 1) * SPAN)
            pieces = [xrecv[0, v, rows, :], xrecv[1, v, rows, :]]
            for side in range(2):
                at = j * SPAN - 1 if side == 0 else (j + 1) * SPAN
                if 0 <= at < span_y:
                    pieces.append(res[v, :, at, :])
                    before = xrecv[0, v, at : at + 1, :]
                    after = xrecv[1, v, at : at + 1, :]
                else:
                    pieces.append(yrecv[side, v])
                    iy = 0 if members == 2 else side
                    cy = 1 - side
                    r0, r1 = 4 + cy * 2 + v, cy * 2 + v
                    before = crecv[0, iy, r0 : r0 + 1, :]
                    after = crecv[1, iy, r1 : r1 + 1, :]
                pieces.append(
                    jnp.where(rim_row == 0, before, jnp.where(rim_row == 1, after, 0.0))
                )
            rests.append(jnp.concatenate(pieces, axis=0))
        hi, lo = split(jnp.concatenate(rests, axis=1))
        hat = part[v] + bdot(fwd[:, 3 * MAIN :][:, : 3 * REST], jnp.concatenate([hi, lo, hi], axis=0))
        stack = jnp.concatenate(
            [hat[:, j * span_z : (j + 1) * span_z] for j in range(count_y)], axis=0
        )
        hi, lo = split(stack)
        spectral = bdot(jnp.concatenate([hi, hi, lo], axis=1), zfwd[...])
        weight = recip[...]
        spectral = spectral * jnp.concatenate([weight] * count_y, axis=0)
        hi, lo = split(spectral)
        both = bdot(hi, zbwd[...])
        back = both[:, :span_z] + both[:, span_z:] + bdot(lo, zbwd[:, 0:span_z])
        solved.append(
            jnp.concatenate([back[j * ROWS : (j + 1) * ROWS] for j in range(count_y)], axis=1)
        )

    updates = []
    if direct:
        everyone = msg.at[pl.ds(0, total - 1)]
        pltpu.make_async_copy(everyone, everyone, all_recv).wait()
        blocks = msg[...]
        whole = pltpu.roll(jnp.sum(blocks, axis=0), half, 1)
        whole = jnp.where(lane8 < half, whole, 0.0)
        blocks = blocks.reshape(groups, members, 8, 2 * half)
        for v in range(vectors):
            terms = jnp.zeros((groups, 8, 2 * half), F32)
            for part_m in range(members):
                at = 4 * part_m + v
                terms = terms + blocks[:, part_m] * whole[at : at + 1, :][None]
            answer = jnp.sum(terms.reshape(groups * 8, 2 * half), axis=1, keepdims=True)
            updates.append(
                [
                    WEIGHT * jnp.sum(answer * member_of[j], axis=0, keepdims=True)
                    for j in range(count_y)
                ]
            )

    stores = []
    for v in range(vectors):
        hi, lo = split(solved[v])
        result = bdot(
            bwd[:, 0 : 3 * MAIN],
            jnp.concatenate([hi[:MAIN], lo[:MAIN], hi[:MAIN]], axis=0),
        ) + bdot(
            bwd[:, 3 * MAIN :][:, : 3 * REST],
            jnp.concatenate([hi[MAIN:], lo[MAIN:], hi[MAIN:]], axis=0),
        )
        for j in range(count_y):
            piece = result[:, j * span_z : (j + 1) * span_z]
            if direct:
                piece = piece + updates[v][j]
            out[v, :, j * SPAN : (j + 1) * SPAN, :] = piece.reshape(SPAN, SPAN, span_z)
        store = pltpu.make_async_copy(out.at[v], out_hbm.at[v], out_sem.at[v])
        store.start()
        stores.append(store)

    for copy in halo:
        copy.wait_send()
    if direct:
        pltpu.make_async_copy(everyone, everyone, all_send).wait()
    for store in stores:
        store.wait()


def on_device(
    residual,
    horiz_vectors,
    horiz_values,
    upward_eigen_tables,
    upward_eigen_values,
    aggregate_map,
    coarse_inverse,
):
    groups = lax.axis_size("group")
    members = lax.axis_size("member")
    vectors, points_x, span_y, span_z = residual.shape
    count_y = span_y // SPAN
    count_z = span_z // SPAN
    total = groups * members
    rows, cols = coarse_inverse.shape
    direct = total <= 64 and members == 2 and rows == 8 and cols == 64 and groups * 8 == 128
    operands = (
        residual,
        jnp.transpose(horiz_vectors, (1, 0, 2)),
        horiz_values,
        jnp.transpose(upward_eigen_tables, (1, 0, 2)),
        upward_eigen_values,
        aggregate_map,
        coarse_inverse,
    )
    corners = 1 if members == 2 else 2
    halos = 4 + 2 * corners
    dma = pltpu.SemaphoreType.DMA
    scratch = [pltpu.VMEM(a.shape, a.dtype) for a in operands]
    scratch += [
        pltpu.VMEM(residual.shape, F32),
        pltpu.VMEM((2, TAIL, 128), F32),
        pltpu.VMEM((8, 128), F32),
        pltpu.VMEM((2, vectors, SPAN, span_z), F32),
        pltpu.VMEM((8, span_z), F32),
        pltpu.VMEM((2, vectors, span_y, span_z), F32),
        pltpu.VMEM((2, vectors, SPAN, span_z), F32),
        pltpu.VMEM((2, corners, 8, span_z), F32),
        pltpu.VMEM((total if direct else 1, 8, 128), F32),
        pltpu.VMEM((8, 128), F32),
        pltpu.VMEM((ROWS, 4 * MAIN), BF16),
        pltpu.VMEM((MAIN, 4 * MAIN), BF16),
        pltpu.VMEM((ROWS, count_z * EXTENT), F32),
        pltpu.VMEM((3 * span_z, count_z * EXTENT), BF16),
        pltpu.VMEM((count_z * EXTENT, 2 * span_z), BF16),
        pltpu.VMEM((vectors, ROWS, count_y * span_z), F32),
        dma((len(operands),)),
        dma((vectors,)),
        dma((halos,)),
        dma((halos,)),
        dma,
        dma,
    ]
    result = pl.pallas_call(
        functools.partial(kernel, groups, members, direct),
        out_shape=jax.ShapeDtypeStruct(residual.shape, F32),
        in_specs=[pl.BlockSpec(memory_space=pltpu.HBM)] * len(operands),
        out_specs=pl.BlockSpec(memory_space=pl.ANY),
        scratch_shapes=scratch,
        compiler_params=pltpu.CompilerParams(
            collective_id=0, has_side_effects=True, vmem_limit_bytes=60 * 1024 * 1024
        ),
        cost_estimate=pl.CostEstimate(
            flops=2 * 10**9, bytes_accessed=2**20, transcendentals=0
        ),
    )(*operands)
    if direct:
        return result
    totals = residual.reshape(vectors, SPAN, count_y, SPAN, count_z, SPAN).sum(axis=(1, 3, 5))
    labels = aggregate_map.reshape(-1)
    partial_rhs = WEIGHT * jax.ops.segment_sum(
        totals.reshape(vectors, -1).T, labels, num_segments=rows * groups
    ).T
    whole_rhs = lax.psum(partial_rhs, ("group", "member"))
    share = lax.dynamic_slice_in_dim(whole_rhs, lax.axis_index("member") * cols, cols, 1)
    row_values = lax.psum(dot(share, coarse_inverse.T), "member")
    coarse = lax.all_gather(row_values, "group", axis=1, tiled=True)
    update = WEIGHT * jnp.take(coarse, labels, axis=1)
    update = update.reshape(vectors, 1, count_y, 1, count_z, 1)
    split_up = (vectors, SPAN, count_y, SPAN, count_z, SPAN)
    return (result.reshape(split_up) + update).reshape(residual.shape)


def solution(mesh):
    in_specs = (
        P(None, "group", "member", None),
        P(),
        P(),
        P(),
        P(),
        P("group", "member", None),
        P("group", "member"),
    )
    out_specs = P(None, "group", "member", None)
    return jax.shard_map(
        on_device, mesh=mesh, in_specs=in_specs, out_specs=out_specs, check_vma=False
    )
```

```python
import functools

import jax
import jax.numpy as jnp
from jax import lax
from jax.experimental import pallas as pl
from jax.experimental.pallas import tpu as pltpu
from jax.sharding import PartitionSpec as P

SPAN = 16
EXTENT = SPAN + 2
MAIN = SPAN * SPAN
TAIL = 24
REST = 2 * SPAN + 2 * TAIL
ROWS = MAIN + REST
WEIGHT = float(SPAN) ** (-1.5)
MESH = pl.DeviceIdType.MESH
F32 = jnp.float32
BF16 = jnp.bfloat16


def iota(shape, dim):
    return lax.broadcasted_iota(jnp.int32, shape, dim)


def dot(a, b):
    return jnp.dot(a, b, precision=lax.Precision.HIGHEST, preferred_element_type=F32)


def dot_t(a, b):
    dims = (((1,), (1,)), ((), ()))
    return lax.dot_general(
        a, b, dims, precision=lax.Precision.HIGHEST, preferred_element_type=F32
    )


def bdot(a, b):
    return jnp.dot(a, b, preferred_element_type=F32)


def bdot_t(a, b):
    dims = (((1,), (1,)), ((), ()))
    return lax.dot_general(a, b, dims, preferred_element_type=F32)


def split(a):
    hi = a.astype(BF16)
    return hi, (a - hi.astype(F32)).astype(BF16)


def choose(a, hot):
    hi, lo = split(a)
    return bdot(hi, hot) + bdot(lo, hot)


def place(hot, a):
    hi, lo = split(a)
    return bdot(hot, hi) + bdot(hot, lo)


def turn(hot, a):
    hi, lo = split(a)
    return bdot_t(hot, hi) + bdot_t(hot, lo)


def hot(condition):
    return condition.astype(F32).astype(BF16)


def high(i):
    return lax.shift_right_logical(i, 4)


def low(i):
    return i & (SPAN - 1)


def rest_of(lane):
    r = lane - MAIN
    r = jnp.where(r >= 2 * REST, r - 2 * REST, jnp.where(r >= REST, r - REST, r))
    t = r - 2 * SPAN
    tail = (t >= 0) & (lane < MAIN + 3 * REST)
    second = t >= TAIL
    return r, tail, second, jnp.where(second, t - TAIL, t)


def point_index(lane):
    r, tail, second, along = rest_of(lane)
    side = jnp.where(r >= SPAN, EXTENT - 1, 0)
    tail_x = jnp.where(
        along < SPAN,
        along + 1,
        jnp.where(along == SPAN, 0, jnp.where(along == SPAN + 1, EXTENT - 1, -1)),
    )
    x = jnp.where(lane < MAIN, 1 + high(lane), jnp.where(tail, tail_x, side))
    y = jnp.where(
        lane < MAIN,
        1 + low(lane),
        jnp.where(tail, jnp.where(second, EXTENT - 1, 0), 1 + low(r)),
    )
    return x, y


def mode_index(lane):
    r, tail, second, along = rest_of(lane)
    a = jnp.where(lane < MAIN, high(lane), jnp.where(tail, along, SPAN + high(r)))
    b = jnp.where(
        lane < MAIN,
        low(lane),
        jnp.where(tail, jnp.where(second, SPAN + 1, SPAN), low(r)),
    )
    return a, b


def store_split(ref, table):
    hi, lo = split(table)
    rows = table.shape[0]
    ref[:, 0:MAIN] = hi[:, :MAIN]
    ref[:, MAIN : 2 * MAIN] = hi[:, :MAIN]
    ref[:, 2 * MAIN : 3 * MAIN] = lo[:, :MAIN]
    lane = iota((rows, MAIN), 1)
    wide = table[:, MAIN:]
    top = wide.astype(BF16).astype(F32)
    mixed = jnp.where(lane < 2 * REST, top, wide - top)
    ref[:, 3 * MAIN :] = jnp.where(lane < 3 * REST, mixed, 0.0).astype(BF16)


def kernel(
    groups,
    members,
    direct,
    res_hbm,
    hvec_hbm,
    hval_hbm,
    ztab_hbm,
    zval_hbm,
    agg_hbm,
    inv_hbm,
    out_hbm,
    res,
    hvec,
    hval,
    ztab,
    zval,
    agg,
    inv,
    out,
    hpad,
    apad,
    ysend,
    csend,
    xrecv,
    yrecv,
    crecv,
    msg,
    box,
    fwd,
    bwd,
    recip,
    zfwd,
    zbwd,
    part,
    in_sem,
    out_sem,
    halo_send,
    halo_recv,
    all_send,
    all_recv,
):
    vectors, _, span_y, span_z = res.shape
    count_y = span_y // SPAN
    count_z = span_z // SPAN
    modes_z = count_z * EXTENT
    total = groups * members
    g = lax.axis_index("group")
    m = lax.axis_index("member")
    me = g * members + m

    def wrap(i, n):
        return jnp.where(i >= n, i - n, i)

    def shifted(dx, dy):
        return (wrap(g + dx % groups, groups), wrap(m + dy % members, members))

    def peers():
        found = [(g, wrap(m + dy, members)) for dy in range(1, members)]
        for dx in range(1, groups):
            other = wrap(g + dx, groups)
            found += [(other, wrap(m + dy, members)) for dy in range(members)]
        return found

    barrier = pltpu.get_barrier_semaphore()
    loads = [
        pltpu.make_async_copy(src, dst, in_sem.at[i])
        for i, (src, dst) in enumerate(
            [
                (res_hbm, res),
                (agg_hbm, agg),
                (inv_hbm, inv),
                (hvec_hbm, hvec),
                (hval_hbm, hval),
                (ztab_hbm, ztab),
                (zval_hbm, zval),
            ]
        )
    ]
    for load in loads:
        load.start()
    corner_dy = (1,) if members == 2 else (1, -1)
    around = [(1, 0), (-1, 0), (0, 1)] + [(0, -1)] * (members > 2)
    around += [(dx, dy) for dx in (1, -1) for dy in corner_dy]
    partners = peers() if direct else [shifted(dx, dy) for dx, dy in around]
    for device in partners:
        pl.semaphore_signal(barrier, inc=1, device_id=device, device_id_type=MESH)
    hpad[...] = jnp.zeros_like(hpad)
    apad[...] = jnp.zeros_like(apad)

    wide = 2 * MAIN
    lane = iota((1, wide), 1)
    row = iota((TAIL, wide), 0)
    eye = hot(iota((TAIL, 128), 0) == iota((TAIL, 128), 1))
    px, py = point_index(lane)
    ma, mb = mode_index(lane)
    px, py, ma, mb = [hot(i == row) for i in (px, py, ma, mb)]
    stacked = count_z * EXTENT
    mode = iota((1, modes_z), 1)
    mode_layer = mode // EXTENT
    mode_inner = mode - EXTENT * mode_layer
    tiled = hot(mode_inner == iota((EXTENT, modes_z), 0))
    zz = iota((span_z, stacked), 0)
    layer = iota((1, stacked), 1) % count_z
    inner = iota((1, stacked), 1) // count_z
    band = hot(zz == SPAN * layer - 1 + inner)
    near = hot((high(zz) == layer) & (inner == low(zz) + 1))
    eye_z = hot(iota((modes_z, modes_z), 0) == iota((modes_z, modes_z), 1))
    row8 = iota((8, span_z), 0)
    spread = hot(high(iota((count_z, span_z), 1)) == iota((count_z, span_z), 0))
    for load in loads[1:]:
        load.wait()

    if direct:
        half = inv.shape[1]
        labels = dot(agg[0].astype(F32), spread.astype(F32))
        row_id = iota((2 * half, span_z), 0).astype(F32)
        member_of = [(labels[j : j + 1, :] == row_id).astype(F32) for j in range(count_y)]
        downward = hot(high(iota((span_z, count_z), 0)) == iota((span_z, count_z), 1))
        upright = dot_t(downward.astype(F32), agg[0].astype(F32))
        lane_id = iota((span_z, 2 * half), 1).astype(F32)
        owned = jnp.concatenate(
            [hot(upright[:, j : j + 1] == lane_id) for j in range(count_y)], axis=0
        )
        apad[:, 0:half] = inv[...]
    loads[0].wait()

    for v in range(vectors):
        ysend[0, v] = res[v, :, span_y - 1, :]
        ysend[1, v] = res[v, :, 0, :]
    for cx in range(2):
        for cy in range(2):
            for v in range(vectors):
                row = cx * 4 + cy * 2 + v
                y_at = (span_y - 1) * cy
                csend[row : row + 1, :] = res[v, (SPAN - 1) * cx, y_at : y_at + 1, :]

    if direct:
        sums = []
        for j in range(count_y):
            placed = jnp.zeros((8, span_z), F32)
            for v in range(vectors):
                tot = jnp.sum(res[v, :, j * SPAN : (j + 1) * SPAN, :], axis=0)
                tot = jnp.sum(tot, axis=0, keepdims=True)
                placed = placed + jnp.where((row8 & 3) == v, tot, 0.0)
            sums.append(placed)
        hi, lo = split(jnp.concatenate(sums, axis=1))
        rhs = WEIGHT * (bdot(hi, owned) + bdot(lo, owned))
        lane8 = iota((8, 2 * half), 1)
        rhs = jnp.where(row8 < 4, pltpu.roll(rhs, half, 1), rhs)
        mine = apad[...] + jnp.where(lane8 < half, 0.0, rhs)
        msg[me] = mine
        box[...] = mine

    halo = []

    def send(src, dst, dx, dy):
        i = len(halo)
        copy = pltpu.make_async_remote_copy(
            src_ref=src,
            dst_ref=dst,
            send_sem=halo_send.at[i],
            recv_sem=halo_recv.at[i],
            device_id=shifted(dx, dy),
            device_id_type=MESH,
        )
        halo.append(copy)

    send(res.at[:, SPAN - 1], xrecv.at[0], 1, 0)
    send(res.at[:, 0], xrecv.at[1], -1, 0)
    for ix, dx in enumerate((1, -1)):
        for iy, dy in enumerate(corner_dy):
            send(csend, crecv.at[ix, iy], dx, dy)
    send(ysend.at[0], yrecv.at[0], 0, 1)
    send(ysend.at[1], yrecv.at[1], 0, -1)

    pl.semaphore_wait(barrier, len(partners))
    for copy in halo:
        copy.start()
    if direct:
        shares = [
            pltpu.make_async_remote_copy(
                src_ref=box,
                dst_ref=msg.at[me],
                send_sem=all_send,
                recv_sem=all_recv,
                device_id=device,
                device_id_type=MESH,
            )
            for device in partners
        ]
        for copy in shares:
            copy.start()

    hpad[0, 0:EXTENT, 0:EXTENT] = hvec[:, 0, :]
    hpad[1, 0:EXTENT, 0:EXTENT] = hvec[:, 1, :]
    xe = choose(turn(eye, hpad[0]), px)
    ye = choose(turn(eye, hpad[1]), py)
    body = xe[:EXTENT][:, None, :] * ye[:SPAN][None, :, :]
    table = jnp.concatenate(
        [
            body.reshape(EXTENT * SPAN, wide),
            xe * ye[SPAN : SPAN + 1, :],
            xe * ye[SPAN + 1 : SPAN + 2, :],
        ],
        axis=0,
    )
    store_split(fwd, table)
    xb = choose(hpad[0, 1 : SPAN + 1, 0:TAIL], ma)
    yb = choose(hpad[1, 1 : SPAN + 1, 0:TAIL], mb)
    store_split(bwd, (xb[:, None, :] * yb[None, :, :]).reshape(MAIN, wide))

    diag = choose(ztab[...].reshape(stacked, EXTENT), tiled)
    diag = jnp.where(mode_layer == iota((stacked, modes_z), 0) % count_z, diag, 0.0)
    hi, lo = split(place(band, diag))
    zfwd[0:span_z, :] = hi
    zfwd[span_z : 2 * span_z, :] = lo
    zfwd[2 * span_z : 3 * span_z, :] = hi
    hi, lo = split(turn(eye_z, place(near, diag)))
    zbwd[:, 0:span_z] = hi
    zbwd[:, span_z : 2 * span_z] = lo

    levels = dot(zval[...], tiled.astype(F32))
    level_own = mode_layer == iota((count_z, modes_z), 0)
    levels = jnp.sum(jnp.where(level_own, levels, 0.0), axis=0, keepdims=True)
    upright_eye = (iota((TAIL, EXTENT), 0) == iota((TAIL, EXTENT), 1)).astype(F32)
    columns = dot_t(upright_eye, hval[...])
    first = jnp.broadcast_to(columns[:, 0:1], (TAIL, modes_z))
    second = columns[:, 1:2] + levels
    body = first[:EXTENT][:, None, :] + second[:SPAN][None, :, :]
    recip[0 : EXTENT * SPAN, :] = 1.0 / body.reshape(EXTENT * SPAN, modes_z)
    for side in range(2):
        rows = slice(EXTENT * SPAN + side * TAIL, EXTENT * SPAN + (side + 1) * TAIL)
        recip[rows, :] = 1.0 / (first + second[SPAN + side : SPAN + side + 1, :])

    for v in range(vectors):
        field = jnp.concatenate(
            [
                res[v, :, j * SPAN : (j + 1) * SPAN, :].reshape(MAIN, span_z)
                for j in range(count_y)
            ],
            axis=1,
        )
        hi, lo = split(field)
        part[v] = bdot(fwd[:, 0 : 3 * MAIN], jnp.concatenate([hi, lo, hi], axis=0))

    for copy in halo:
        copy.wait_recv()

    rim_row = iota((8, span_z), 0)
    solved = []
    for v in range(vectors):
        rests = []
        for j in range(count_y):
            rows = slice(j * SPAN, (j + 1) * SPAN)
            pieces = [xrecv[0, v, rows, :], xrecv[1, v, rows, :]]
            for side in range(2):
                at = j * SPAN - 1 if side == 0 else (j + 1) * SPAN
                if 0 <= at < span_y:
                    pieces.append(res[v, :, at, :])
                    before = xrecv[0, v, at : at + 1, :]
                    after = xrecv[1, v, at : at + 1, :]
                else:
                    pieces.append(yrecv[side, v])
                    iy = 0 if members == 2 else side
                    cy = 1 - side
                    r0, r1 = 4 + cy * 2 + v, cy * 2 + v
                    before = crecv[0, iy, r0 : r0 + 1, :]
                    after = crecv[1, iy, r1 : r1 + 1, :]
                pieces.append(
                    jnp.where(rim_row == 0, before, jnp.where(rim_row == 1, after, 0.0))
                )
            rests.append(jnp.concatenate(pieces, axis=0))
        hi, lo = split(jnp.concatenate(rests, axis=1))
        hat = part[v] + bdot(fwd[:, 3 * MAIN :][:, : 3 * REST], jnp.concatenate([hi, lo, hi], axis=0))
        stack = jnp.concatenate(
            [hat[:, j * span_z : (j + 1) * span_z] for j in range(count_y)], axis=0
        )
        hi, lo = split(stack)
        spectral = bdot(jnp.concatenate([hi, hi, lo], axis=1), zfwd[...])
        weight = recip[...]
        spectral = spectral * jnp.concatenate([weight] * count_y, axis=0)
        hi, lo = split(spectral)
        both = bdot(hi, zbwd[...])
        back = both[:, :span_z] + both[:, span_z:] + bdot(lo, zbwd[:, 0:span_z])
        solved.append(
            jnp.concatenate([back[j * ROWS : (j + 1) * ROWS] for j in range(count_y)], axis=1)
        )

    updates = []
    if direct:
        everyone = msg.at[pl.ds(0, total - 1)]
        pltpu.make_async_copy(everyone, everyone, all_recv).wait()
        blocks = msg[...]
        whole = pltpu.roll(jnp.sum(blocks, axis=0), half, 1)
        whole = jnp.where(lane8 < half, whole, 0.0)
        blocks = blocks.reshape(groups, members, 8, 2 * half)
        for v in range(vectors):
            terms = jnp.zeros((groups, 8, 2 * half), F32)
            for part_m in range(members):
                at = 4 * part_m + v
                terms = terms + blocks[:, part_m] * whole[at : at + 1, :][None]
            answer = jnp.sum(terms.reshape(groups * 8, 2 * half), axis=1, keepdims=True)
            updates.append(
                [
                    WEIGHT * jnp.sum(answer * member_of[j], axis=0, keepdims=True)
                    for j in range(count_y)
                ]
            )

    stores = []
    for v in range(vectors):
        hi, lo = split(solved[v])
        result = bdot(
            bwd[:, 0 : 3 * MAIN],
            jnp.concatenate([hi[:MAIN], lo[:MAIN], hi[:MAIN]], axis=0),
        ) + bdot(
            bwd[:, 3 * MAIN :][:, : 3 * REST],
            jnp.concatenate([hi[MAIN:], lo[MAIN:], hi[MAIN:]], axis=0),
        )
        for j in range(count_y):
            piece = result[:, j * span_z : (j + 1) * span_z]
            if direct:
                piece = piece + updates[v][j]
            out[v, :, j * SPAN : (j + 1) * SPAN, :] = piece.reshape(SPAN, SPAN, span_z)
        store = pltpu.make_async_copy(out.at[v], out_hbm.at[v], out_sem.at[v])
        store.start()
        stores.append(store)

    for copy in halo:
        copy.wait_send()
    if direct:
        pltpu.make_async_copy(everyone, everyone, all_send).wait()
    for store in stores:
        store.wait()


def hand_over(src, dst, sem):
    vectors, points_x = src.shape[:2]
    pieces = sem.shape[0] // vectors
    depth = points_x // pieces
    copies = []
    for v in range(vectors):
        for i in range(pieces):
            rows = pl.ds(i * depth, depth)
            copies.append(
                pltpu.make_async_copy(
                    src.at[v, rows], dst.at[v, rows], sem.at[v * pieces + i]
                )
            )
    for copy in copies:
        copy.start()
    for copy in copies:
        copy.wait()


def on_device(
    residual,
    horiz_vectors,
    horiz_values,
    upward_eigen_tables,
    upward_eigen_values,
    aggregate_map,
    coarse_inverse,
):
    groups = lax.axis_size("group")
    members = lax.axis_size("member")
    vectors, points_x, span_y, span_z = residual.shape
    count_y = span_y // SPAN
    count_z = span_z // SPAN
    total = groups * members
    rows, cols = coarse_inverse.shape
    direct = total <= 64 and members == 2 and rows == 8 and cols == 64 and groups * 8 == 128
    operands = (
        residual,
        jnp.transpose(horiz_vectors, (1, 0, 2)),
        horiz_values,
        jnp.transpose(upward_eigen_tables, (1, 0, 2)),
        upward_eigen_values,
        aggregate_map,
        coarse_inverse,
    )
    corners = 1 if members == 2 else 2
    halos = 4 + 2 * corners
    dma = pltpu.SemaphoreType.DMA
    scratch = [pltpu.VMEM(a.shape, a.dtype) for a in operands]
    scratch += [
        pltpu.VMEM(residual.shape, F32),
        pltpu.VMEM((2, TAIL, 128), F32),
        pltpu.VMEM((8, 128), F32),
        pltpu.VMEM((2, vectors, SPAN, span_z), F32),
        pltpu.VMEM((8, span_z), F32),
        pltpu.VMEM((2, vectors, span_y, span_z), F32),
        pltpu.VMEM((2, vectors, SPAN, span_z), F32),
        pltpu.VMEM((2, corners, 8, span_z), F32),
        pltpu.VMEM((total if direct else 1, 8, 128), F32),
        pltpu.VMEM((8, 128), F32),
        pltpu.VMEM((ROWS, 4 * MAIN), BF16),
        pltpu.VMEM((MAIN, 4 * MAIN), BF16),
        pltpu.VMEM((ROWS, count_z * EXTENT), F32),
        pltpu.VMEM((3 * span_z, count_z * EXTENT), BF16),
        pltpu.VMEM((count_z * EXTENT, 2 * span_z), BF16),
        pltpu.VMEM((vectors, ROWS, count_y * span_z), F32),
        dma((len(operands),)),
        dma((vectors,)),
        dma((halos,)),
        dma((halos,)),
        dma,
        dma,
    ]
    result = pl.pallas_call(
        functools.partial(kernel, groups, members, direct),
        out_shape=jax.ShapeDtypeStruct(residual.shape, F32),
        in_specs=[pl.BlockSpec(memory_space=pltpu.HBM)] * len(operands),
        out_specs=pl.BlockSpec(memory_space=pl.ANY),
        scratch_shapes=scratch,
        compiler_params=pltpu.CompilerParams(
            collective_id=0, has_side_effects=True, vmem_limit_bytes=60 * 1024 * 1024
        ),
        cost_estimate=pl.CostEstimate(
            flops=2 * 10**9, bytes_accessed=2**20, transcendentals=0
        ),
    )(*operands)
    if direct:
        return pl.pallas_call(
            hand_over,
            out_shape=jax.ShapeDtypeStruct(residual.shape, F32),
            in_specs=[pl.BlockSpec(memory_space=pltpu.HBM)],
            out_specs=pl.BlockSpec(memory_space=pltpu.HBM),
            scratch_shapes=[dma((4 * vectors,))],
            compiler_params=pltpu.CompilerParams(vmem_limit_bytes=60 * 1024 * 1024),
        )(result)
    totals = residual.reshape(vectors, SPAN, count_y, SPAN, count_z, SPAN).sum(axis=(1, 3, 5))
    labels = aggregate_map.reshape(-1)
    partial_rhs = WEIGHT * jax.ops.segment_sum(
        totals.reshape(vectors, -1).T, labels, num_segments=rows * groups
    ).T
    whole_rhs = lax.psum(partial_rhs, ("group", "member"))
    share = lax.dynamic_slice_in_dim(whole_rhs, lax.axis_index("member") * cols, cols, 1)
    row_values = lax.psum(dot(share, coarse_inverse.T), "member")
    coarse = lax.all_gather(row_values, "group", axis=1, tiled=True)
    update = WEIGHT * jnp.take(coarse, labels, axis=1)
    update = update.reshape(vectors, 1, count_y, 1, count_z, 1)
    split_up = (vectors, SPAN, count_y, SPAN, count_z, SPAN)
    return (result.reshape(split_up) + update).reshape(residual.shape)


def solution(mesh):
    in_specs = (
        P(None, "group", "member", None),
        P(),
        P(),
        P(),
        P(),
        P("group", "member", None),
        P("group", "member"),
    )
    out_specs = P(None, "group", "member", None)
    return jax.shard_map(
        on_device, mesh=mesh, in_specs=in_specs, out_specs=out_specs, check_vma=False
    )
```

```python
import functools

import jax
import jax.numpy as jnp
from jax import lax
from jax.experimental import pallas as pl
from jax.experimental.pallas import tpu as pltpu
from jax.sharding import PartitionSpec as P

SPAN = 16
EXTENT = SPAN + 2
MAIN = SPAN * SPAN
TAIL = 24
REST = 2 * SPAN + 2 * TAIL
ROWS = MAIN + REST
WEIGHT = float(SPAN) ** (-1.5)
MESH = pl.DeviceIdType.MESH
F32 = jnp.float32
BF16 = jnp.bfloat16


def iota(shape, dim):
    return lax.broadcasted_iota(jnp.int32, shape, dim)


def dot(a, b):
    return jnp.dot(a, b, precision=lax.Precision.HIGHEST, preferred_element_type=F32)


def dot_t(a, b):
    dims = (((1,), (1,)), ((), ()))
    return lax.dot_general(
        a, b, dims, precision=lax.Precision.HIGHEST, preferred_element_type=F32
    )


def bdot(a, b):
    return jnp.dot(a, b, preferred_element_type=F32)


def bdot_t(a, b):
    dims = (((1,), (1,)), ((), ()))
    return lax.dot_general(a, b, dims, preferred_element_type=F32)


def split(a):
    hi = a.astype(BF16)
    return hi, (a - hi.astype(F32)).astype(BF16)


def choose(a, hot):
    hi, lo = split(a)
    return bdot(hi, hot) + bdot(lo, hot)


def place(hot, a):
    hi, lo = split(a)
    return bdot(hot, hi) + bdot(hot, lo)


def turn(hot, a):
    hi, lo = split(a)
    return bdot_t(hot, hi) + bdot_t(hot, lo)


def hot(condition):
    return condition.astype(F32).astype(BF16)


def high(i):
    return lax.shift_right_logical(i, 4)


def low(i):
    return i & (SPAN - 1)


def rest_of(lane):
    r = lane - MAIN
    r = jnp.where(r >= 2 * REST, r - 2 * REST, jnp.where(r >= REST, r - REST, r))
    t = r - 2 * SPAN
    tail = (t >= 0) & (lane < MAIN + 3 * REST)
    second = t >= TAIL
    return r, tail, second, jnp.where(second, t - TAIL, t)


def point_index(lane):
    r, tail, second, along = rest_of(lane)
    side = jnp.where(r >= SPAN, EXTENT - 1, 0)
    tail_x = jnp.where(
        along < SPAN,
        along + 1,
        jnp.where(along == SPAN, 0, jnp.where(along == SPAN + 1, EXTENT - 1, -1)),
    )
    x = jnp.where(lane < MAIN, 1 + high(lane), jnp.where(tail, tail_x, side))
    y = jnp.where(
        lane < MAIN,
        1 + low(lane),
        jnp.where(tail, jnp.where(second, EXTENT - 1, 0), 1 + low(r)),
    )
    return x, y


def mode_index(lane):
    r, tail, second, along = rest_of(lane)
    a = jnp.where(lane < MAIN, high(lane), jnp.where(tail, along, SPAN + high(r)))
    b = jnp.where(
        lane < MAIN,
        low(lane),
        jnp.where(tail, jnp.where(second, SPAN + 1, SPAN), low(r)),
    )
    return a, b


def store_split(ref, table):
    hi, lo = split(table)
    rows = table.shape[0]
    ref[:, 0:MAIN] = hi[:, :MAIN]
    ref[:, MAIN : 2 * MAIN] = hi[:, :MAIN]
    ref[:, 2 * MAIN : 3 * MAIN] = lo[:, :MAIN]
    lane = iota((rows, MAIN), 1)
    wide = table[:, MAIN:]
    top = wide.astype(BF16).astype(F32)
    mixed = jnp.where(lane < 2 * REST, top, wide - top)
    ref[:, 3 * MAIN :] = jnp.where(lane < 3 * REST, mixed, 0.0).astype(BF16)


def kernel(
    groups,
    members,
    direct,
    res_hbm,
    hvec_hbm,
    hval_hbm,
    ztab_hbm,
    zval_hbm,
    agg_hbm,
    inv_hbm,
    out_hbm,
    res,
    hvec,
    hval,
    ztab,
    zval,
    agg,
    inv,
    out,
    hpad,
    apad,
    ysend,
    csend,
    xrecv,
    yrecv,
    crecv,
    msg,
    box,
    fwd,
    bwd,
    recip,
    zfwd,
    zbwd,
    part,
    in_sem,
    out_sem,
    halo_send,
    halo_recv,
    all_send,
    all_recv,
):
    vectors, _, span_y, span_z = res.shape
    count_y = span_y // SPAN
    count_z = span_z // SPAN
    modes_z = count_z * EXTENT
    total = groups * members
    g = lax.axis_index("group")
    m = lax.axis_index("member")
    me = g * members + m

    def wrap(i, n):
        return jnp.where(i >= n, i - n, i)

    def shifted(dx, dy):
        return (wrap(g + dx % groups, groups), wrap(m + dy % members, members))

    def peers():
        found = [(g, wrap(m + dy, members)) for dy in range(1, members)]
        for dx in range(1, groups):
            other = wrap(g + dx, groups)
            found += [(other, wrap(m + dy, members)) for dy in range(members)]
        return found

    barrier = pltpu.get_barrier_semaphore()
    loads = [
        pltpu.make_async_copy(src, dst, in_sem.at[i])
        for i, (src, dst) in enumerate(
            [
                (res_hbm, res),
                (agg_hbm, agg),
                (inv_hbm, inv),
                (hvec_hbm, hvec),
                (hval_hbm, hval),
                (ztab_hbm, ztab),
                (zval_hbm, zval),
            ]
        )
    ]
    for load in loads:
        load.start()
    corner_dy = (1,) if members == 2 else (1, -1)
    around = [(1, 0), (-1, 0), (0, 1)] + [(0, -1)] * (members > 2)
    around += [(dx, dy) for dx in (1, -1) for dy in corner_dy]
    partners = peers() if direct else [shifted(dx, dy) for dx, dy in around]
    for device in partners:
        pl.semaphore_signal(barrier, inc=1, device_id=device, device_id_type=MESH)
    hpad[...] = jnp.zeros_like(hpad)
    apad[...] = jnp.zeros_like(apad)

    wide = 2 * MAIN
    lane = iota((1, wide), 1)
    row = iota((TAIL, wide), 0)
    eye = hot(iota((TAIL, 128), 0) == iota((TAIL, 128), 1))
    px, py = point_index(lane)
    ma, mb = mode_index(lane)
    px, py, ma, mb = [hot(i == row) for i in (px, py, ma, mb)]
    stacked = count_z * EXTENT
    mode = iota((1, modes_z), 1)
    mode_layer = mode // EXTENT
    mode_inner = mode - EXTENT * mode_layer
    tiled = hot(mode_inner == iota((EXTENT, modes_z), 0))
    zz = iota((span_z, stacked), 0)
    layer = iota((1, stacked), 1) % count_z
    inner = iota((1, stacked), 1) // count_z
    band = hot(zz == SPAN * layer - 1 + inner)
    near = hot((high(zz) == layer) & (inner == low(zz) + 1))
    eye_z = hot(iota((modes_z, modes_z), 0) == iota((modes_z, modes_z), 1))
    row8 = iota((8, span_z), 0)
    spread = hot(high(iota((count_z, span_z), 1)) == iota((count_z, span_z), 0))
    for load in loads[1:]:
        load.wait()

    if direct:
        half = inv.shape[1]
        labels = dot(agg[0].astype(F32), spread.astype(F32))
        row_id = iota((2 * half, span_z), 0).astype(F32)
        member_of = [(labels[j : j + 1, :] == row_id).astype(F32) for j in range(count_y)]
        downward = hot(high(iota((span_z, count_z), 0)) == iota((span_z, count_z), 1))
        upright = dot_t(downward.astype(F32), agg[0].astype(F32))
        lane_id = iota((span_z, 2 * half), 1).astype(F32)
        owned = jnp.concatenate(
            [hot(upright[:, j : j + 1] == lane_id) for j in range(count_y)], axis=0
        )
        apad[:, 0:half] = inv[...]
    diag = choose(ztab[...].reshape(stacked, EXTENT), tiled)
    diag = jnp.where(mode_layer == iota((stacked, modes_z), 0) % count_z, diag, 0.0)
    hi, lo = split(place(band, diag))
    zfwd[0:span_z, :] = hi
    zfwd[span_z : 2 * span_z, :] = lo
    zfwd[2 * span_z : 3 * span_z, :] = hi
    hi, lo = split(turn(eye_z, place(near, diag)))
    zbwd[:, 0:span_z] = hi
    zbwd[:, span_z : 2 * span_z] = lo

    levels = dot(zval[...], tiled.astype(F32))
    level_own = mode_layer == iota((count_z, modes_z), 0)
    levels = jnp.sum(jnp.where(level_own, levels, 0.0), axis=0, keepdims=True)
    upright_eye = (iota((TAIL, EXTENT), 0) == iota((TAIL, EXTENT), 1)).astype(F32)
    columns = dot_t(upright_eye, hval[...])
    first = jnp.broadcast_to(columns[:, 0:1], (TAIL, modes_z))
    second = columns[:, 1:2] + levels
    body = first[:EXTENT][:, None, :] + second[:SPAN][None, :, :]
    recip[0 : EXTENT * SPAN, :] = 1.0 / body.reshape(EXTENT * SPAN, modes_z)
    for side in range(2):
        rows = slice(EXTENT * SPAN + side * TAIL, EXTENT * SPAN + (side + 1) * TAIL)
        recip[rows, :] = 1.0 / (first + second[SPAN + side : SPAN + side + 1, :])

    loads[0].wait()

    for v in range(vectors):
        ysend[0, v] = res[v, :, span_y - 1, :]
        ysend[1, v] = res[v, :, 0, :]
    for cx in range(2):
        for cy in range(2):
            for v in range(vectors):
                row = cx * 4 + cy * 2 + v
                y_at = (span_y - 1) * cy
                csend[row : row + 1, :] = res[v, (SPAN - 1) * cx, y_at : y_at + 1, :]

    if direct:
        sums = []
        for j in range(count_y):
            placed = jnp.zeros((8, span_z), F32)
            for v in range(vectors):
                tot = jnp.sum(res[v, :, j * SPAN : (j + 1) * SPAN, :], axis=0)
                tot = jnp.sum(tot, axis=0, keepdims=True)
                placed = placed + jnp.where((row8 & 3) == v, tot, 0.0)
            sums.append(placed)
        hi, lo = split(jnp.concatenate(sums, axis=1))
        rhs = WEIGHT * (bdot(hi, owned) + bdot(lo, owned))
        lane8 = iota((8, 2 * half), 1)
        rhs = jnp.where(row8 < 4, pltpu.roll(rhs, half, 1), rhs)
        mine = apad[...] + jnp.where(lane8 < half, 0.0, rhs)
        msg[me] = mine
        box[...] = mine

    halo = []

    def send(src, dst, dx, dy):
        i = len(halo)
        copy = pltpu.make_async_remote_copy(
            src_ref=src,
            dst_ref=dst,
            send_sem=halo_send.at[i],
            recv_sem=halo_recv.at[i],
            device_id=shifted(dx, dy),
            device_id_type=MESH,
        )
        halo.append(copy)

    send(res.at[:, SPAN - 1], xrecv.at[0], 1, 0)
    send(res.at[:, 0], xrecv.at[1], -1, 0)
    for ix, dx in enumerate((1, -1)):
        for iy, dy in enumerate(corner_dy):
            send(csend, crecv.at[ix, iy], dx, dy)
    send(ysend.at[0], yrecv.at[0], 0, 1)
    send(ysend.at[1], yrecv.at[1], 0, -1)

    pl.semaphore_wait(barrier, len(partners))
    for copy in halo:
        copy.start()
    if direct:
        shares = [
            pltpu.make_async_remote_copy(
                src_ref=box,
                dst_ref=msg.at[me],
                send_sem=all_send,
                recv_sem=all_recv,
                device_id=device,
                device_id_type=MESH,
            )
            for device in partners
        ]
        for copy in shares:
            copy.start()

    hpad[0, 0:EXTENT, 0:EXTENT] = hvec[:, 0, :]
    hpad[1, 0:EXTENT, 0:EXTENT] = hvec[:, 1, :]
    xe = choose(turn(eye, hpad[0]), px)
    ye = choose(turn(eye, hpad[1]), py)
    body = xe[:EXTENT][:, None, :] * ye[:SPAN][None, :, :]
    table = jnp.concatenate(
        [
            body.reshape(EXTENT * SPAN, wide),
            xe * ye[SPAN : SPAN + 1, :],
            xe * ye[SPAN + 1 : SPAN + 2, :],
        ],
        axis=0,
    )
    store_split(fwd, table)
    xb = choose(hpad[0, 1 : SPAN + 1, 0:TAIL], ma)
    yb = choose(hpad[1, 1 : SPAN + 1, 0:TAIL], mb)
    store_split(bwd, (xb[:, None, :] * yb[None, :, :]).reshape(MAIN, wide))

    for v in range(vectors):
        field = jnp.concatenate(
            [
                res[v, :, j * SPAN : (j + 1) * SPAN, :].reshape(MAIN, span_z)
                for j in range(count_y)
            ],
            axis=1,
        )
        hi, lo = split(field)
        part[v] = bdot(fwd[:, 0 : 3 * MAIN], jnp.concatenate([hi, lo, hi], axis=0))

    for copy in halo:
        copy.wait_recv()

    rim_row = iota((8, span_z), 0)
    solved = []
    for v in range(vectors):
        rests = []
        for j in range(count_y):
            rows = slice(j * SPAN, (j + 1) * SPAN)
            pieces = [xrecv[0, v, rows, :], xrecv[1, v, rows, :]]
            for side in range(2):
                at = j * SPAN - 1 if side == 0 else (j + 1) * SPAN
                if 0 <= at < span_y:
                    pieces.append(res[v, :, at, :])
                    before = xrecv[0, v, at : at + 1, :]
                    after = xrecv[1, v, at : at + 1, :]
                else:
                    pieces.append(yrecv[side, v])
                    iy = 0 if members == 2 else side
                    cy = 1 - side
                    r0, r1 = 4 + cy * 2 + v, cy * 2 + v
                    before = crecv[0, iy, r0 : r0 + 1, :]
                    after = crecv[1, iy, r1 : r1 + 1, :]
                pieces.append(
                    jnp.where(rim_row == 0, before, jnp.where(rim_row == 1, after, 0.0))
                )
            rests.append(jnp.concatenate(pieces, axis=0))
        hi, lo = split(jnp.concatenate(rests, axis=1))
        hat = part[v] + bdot(fwd[:, 3 * MAIN :][:, : 3 * REST], jnp.concatenate([hi, lo, hi], axis=0))
        stack = jnp.concatenate(
            [hat[:, j * span_z : (j + 1) * span_z] for j in range(count_y)], axis=0
        )
        hi, lo = split(stack)
        spectral = bdot(jnp.concatenate([hi, hi, lo], axis=1), zfwd[...])
        weight = recip[...]
        spectral = spectral * jnp.concatenate([weight] * count_y, axis=0)
        hi, lo = split(spectral)
        both = bdot(hi, zbwd[...])
        back = both[:, :span_z] + both[:, span_z:] + bdot(lo, zbwd[:, 0:span_z])
        solved.append(
            jnp.concatenate([back[j * ROWS : (j + 1) * ROWS] for j in range(count_y)], axis=1)
        )

    updates = []
    if direct:
        everyone = msg.at[pl.ds(0, total - 1)]
        pltpu.make_async_copy(everyone, everyone, all_recv).wait()
        blocks = msg[...]
        whole = pltpu.roll(jnp.sum(blocks, axis=0), half, 1)
        whole = jnp.where(lane8 < half, whole, 0.0)
        blocks = blocks.reshape(groups, members, 8, 2 * half)
        for v in range(vectors):
            terms = jnp.zeros((groups, 8, 2 * half), F32)
            for part_m in range(members):
                at = 4 * part_m + v
                terms = terms + blocks[:, part_m] * whole[at : at + 1, :][None]
            answer = jnp.sum(terms.reshape(groups * 8, 2 * half), axis=1, keepdims=True)
            updates.append(
                [
                    WEIGHT * jnp.sum(answer * member_of[j], axis=0, keepdims=True)
                    for j in range(count_y)
                ]
            )

    stores = []
    for v in range(vectors):
        hi, lo = split(solved[v])
        main_part = jnp.concatenate([hi[:MAIN], lo[:MAIN], hi[:MAIN]], axis=0)
        rest_part = jnp.concatenate([hi[MAIN:], lo[MAIN:], hi[MAIN:]], axis=0)
        for piece_x in range(2):
            rows = slice(piece_x * MAIN // 2, (piece_x + 1) * MAIN // 2)
            points = slice(piece_x * SPAN // 2, (piece_x + 1) * SPAN // 2)
            result = bdot(bwd[rows, 0 : 3 * MAIN], main_part) + bdot(
                bwd[rows, 3 * MAIN :][:, : 3 * REST], rest_part
            )
            for j in range(count_y):
                piece = result[:, j * span_z : (j + 1) * span_z]
                if direct:
                    piece = piece + updates[v][j]
                out[v, points, j * SPAN : (j + 1) * SPAN, :] = piece.reshape(
                    SPAN // 2, SPAN, span_z
                )
            store = pltpu.make_async_copy(
                out.at[v, points], out_hbm.at[v, points], out_sem.at[2 * v + piece_x]
            )
            store.start()
            stores.append(store)

    for copy in halo:
        copy.wait_send()
    if direct:
        pltpu.make_async_copy(everyone, everyone, all_send).wait()
    for store in stores:
        store.wait()


def on_device(
    residual,
    horiz_vectors,
    horiz_values,
    upward_eigen_tables,
    upward_eigen_values,
    aggregate_map,
    coarse_inverse,
):
    groups = lax.axis_size("group")
    members = lax.axis_size("member")
    vectors, points_x, span_y, span_z = residual.shape
    count_y = span_y // SPAN
    count_z = span_z // SPAN
    total = groups * members
    rows, cols = coarse_inverse.shape
    direct = total <= 64 and members == 2 and rows == 8 and cols == 64 and groups * 8 == 128
    operands = (
        residual,
        jnp.transpose(horiz_vectors, (1, 0, 2)),
        horiz_values,
        jnp.transpose(upward_eigen_tables, (1, 0, 2)),
        upward_eigen_values,
        aggregate_map,
        coarse_inverse,
    )
    corners = 1 if members == 2 else 2
    halos = 4 + 2 * corners
    dma = pltpu.SemaphoreType.DMA
    scratch = [pltpu.VMEM(a.shape, a.dtype) for a in operands]
    scratch += [
        pltpu.VMEM(residual.shape, F32),
        pltpu.VMEM((2, TAIL, 128), F32),
        pltpu.VMEM((8, 128), F32),
        pltpu.VMEM((2, vectors, SPAN, span_z), F32),
        pltpu.VMEM((8, span_z), F32),
        pltpu.VMEM((2, vectors, span_y, span_z), F32),
        pltpu.VMEM((2, vectors, SPAN, span_z), F32),
        pltpu.VMEM((2, corners, 8, span_z), F32),
        pltpu.VMEM((total if direct else 1, 8, 128), F32),
        pltpu.VMEM((8, 128), F32),
        pltpu.VMEM((ROWS, 4 * MAIN), BF16),
        pltpu.VMEM((MAIN, 4 * MAIN), BF16),
        pltpu.VMEM((ROWS, count_z * EXTENT), F32),
        pltpu.VMEM((3 * span_z, count_z * EXTENT), BF16),
        pltpu.VMEM((count_z * EXTENT, 2 * span_z), BF16),
        pltpu.VMEM((vectors, ROWS, count_y * span_z), F32),
        dma((len(operands),)),
        dma((2 * vectors,)),
        dma((halos,)),
        dma((halos,)),
        dma,
        dma,
    ]
    result = pl.pallas_call(
        functools.partial(kernel, groups, members, direct),
        out_shape=jax.ShapeDtypeStruct(residual.shape, F32),
        in_specs=[pl.BlockSpec(memory_space=pltpu.HBM)] * len(operands),
        out_specs=pl.BlockSpec(memory_space=pl.ANY),
        scratch_shapes=scratch,
        compiler_params=pltpu.CompilerParams(
            collective_id=0, has_side_effects=True, vmem_limit_bytes=60 * 1024 * 1024
        ),
        cost_estimate=pl.CostEstimate(
            flops=2 * 10**9, bytes_accessed=2**20, transcendentals=0
        ),
    )(*operands)
    if direct:
        return result
    totals = residual.reshape(vectors, SPAN, count_y, SPAN, count_z, SPAN).sum(axis=(1, 3, 5))
    labels = aggregate_map.reshape(-1)
    partial_rhs = WEIGHT * jax.ops.segment_sum(
        totals.reshape(vectors, -1).T, labels, num_segments=rows * groups
    ).T
    whole_rhs = lax.psum(partial_rhs, ("group", "member"))
    share = lax.dynamic_slice_in_dim(whole_rhs, lax.axis_index("member") * cols, cols, 1)
    row_values = lax.psum(dot(share, coarse_inverse.T), "member")
    coarse = lax.all_gather(row_values, "group", axis=1, tiled=True)
    update = WEIGHT * jnp.take(coarse, labels, axis=1)
    update = update.reshape(vectors, 1, count_y, 1, count_z, 1)
    split_up = (vectors, SPAN, count_y, SPAN, count_z, SPAN)
    return (result.reshape(split_up) + update).reshape(residual.shape)


def solution(mesh):
    in_specs = (
        P(None, "group", "member", None),
        P(),
        P(),
        P(),
        P(),
        P("group", "member", None),
        P("group", "member"),
    )
    out_specs = P(None, "group", "member", None)
    return jax.shard_map(
        on_device, mesh=mesh, in_specs=in_specs, out_specs=out_specs, check_vma=False
    )
```

```python
import functools

import jax
import jax.numpy as jnp
from jax import lax
from jax.experimental import pallas as pl
from jax.experimental.pallas import tpu as pltpu
from jax.sharding import PartitionSpec as P

SPAN = 16
EXTENT = SPAN + 2
MAIN = SPAN * SPAN
TAIL = 24
REST = 2 * SPAN + 2 * TAIL
ROWS = MAIN + REST
WEIGHT = float(SPAN) ** (-1.5)
MESH = pl.DeviceIdType.MESH
F32 = jnp.float32
BF16 = jnp.bfloat16


def iota(shape, dim):
    return lax.broadcasted_iota(jnp.int32, shape, dim)


def dot(a, b):
    return jnp.dot(a, b, precision=lax.Precision.HIGHEST, preferred_element_type=F32)


def dot_t(a, b):
    dims = (((1,), (1,)), ((), ()))
    return lax.dot_general(
        a, b, dims, precision=lax.Precision.HIGHEST, preferred_element_type=F32
    )


def bdot(a, b):
    return jnp.dot(a, b, preferred_element_type=F32)


def bdot_t(a, b):
    dims = (((1,), (1,)), ((), ()))
    return lax.dot_general(a, b, dims, preferred_element_type=F32)


def split(a):
    hi = a.astype(BF16)
    return hi, (a - hi.astype(F32)).astype(BF16)


def choose(a, hot):
    hi, lo = split(a)
    return bdot(hi, hot) + bdot(lo, hot)


def place(hot, a):
    hi, lo = split(a)
    return bdot(hot, hi) + bdot(hot, lo)


def turn(hot, a):
    hi, lo = split(a)
    return bdot_t(hot, hi) + bdot_t(hot, lo)


def hot(condition):
    return condition.astype(F32).astype(BF16)


def high(i):
    return lax.shift_right_logical(i, 4)


def low(i):
    return i & (SPAN - 1)


def rest_of(lane):
    r = lane - MAIN
    r = jnp.where(r >= 2 * REST, r - 2 * REST, jnp.where(r >= REST, r - REST, r))
    t = r - 2 * SPAN
    tail = (t >= 0) & (lane < MAIN + 3 * REST)
    second = t >= TAIL
    return r, tail, second, jnp.where(second, t - TAIL, t)


def point_index(lane):
    r, tail, second, along = rest_of(lane)
    side = jnp.where(r >= SPAN, EXTENT - 1, 0)
    tail_x = jnp.where(
        along < SPAN,
        along + 1,
        jnp.where(along == SPAN, 0, jnp.where(along == SPAN + 1, EXTENT - 1, -1)),
    )
    x = jnp.where(lane < MAIN, 1 + high(lane), jnp.where(tail, tail_x, side))
    y = jnp.where(
        lane < MAIN,
        1 + low(lane),
        jnp.where(tail, jnp.where(second, EXTENT - 1, 0), 1 + low(r)),
    )
    return x, y


def mode_index(lane):
    r, tail, second, along = rest_of(lane)
    a = jnp.where(lane < MAIN, high(lane), jnp.where(tail, along, SPAN + high(r)))
    b = jnp.where(
        lane < MAIN,
        low(lane),
        jnp.where(tail, jnp.where(second, SPAN + 1, SPAN), low(r)),
    )
    return a, b


def store_split(ref, table):
    hi, lo = split(table)
    rows = table.shape[0]
    ref[:, 0:MAIN] = hi[:, :MAIN]
    ref[:, MAIN : 2 * MAIN] = hi[:, :MAIN]
    ref[:, 2 * MAIN : 3 * MAIN] = lo[:, :MAIN]
    lane = iota((rows, MAIN), 1)
    wide = table[:, MAIN:]
    top = wide.astype(BF16).astype(F32)
    mixed = jnp.where(lane < 2 * REST, top, wide - top)
    ref[:, 3 * MAIN :] = jnp.where(lane < 3 * REST, mixed, 0.0).astype(BF16)


def kernel(
    groups,
    members,
    direct,
    res_hbm,
    hvec_hbm,
    hval_hbm,
    ztab_hbm,
    zval_hbm,
    agg_hbm,
    inv_hbm,
    out_hbm,
    res,
    hvec,
    hval,
    ztab,
    zval,
    agg,
    inv,
    out,
    hpad,
    apad,
    ysend,
    csend,
    xrecv,
    yrecv,
    crecv,
    msg,
    box,
    fwd,
    bwd,
    recip,
    zfwd,
    zbwd,
    part,
    in_sem,
    out_sem,
    halo_send,
    halo_recv,
    all_send,
    all_recv,
):
    vectors, _, span_y, span_z = res.shape
    count_y = span_y // SPAN
    count_z = span_z // SPAN
    modes_z = count_z * EXTENT
    total = groups * members
    g = lax.axis_index("group")
    m = lax.axis_index("member")
    me = g * members + m

    def wrap(i, n):
        return jnp.where(i >= n, i - n, i)

    def shifted(dx, dy):
        return (wrap(g + dx % groups, groups), wrap(m + dy % members, members))

    def peers():
        found = [(g, wrap(m + dy, members)) for dy in range(1, members)]
        for dx in range(1, groups):
            other = wrap(g + dx, groups)
            found += [(other, wrap(m + dy, members)) for dy in range(members)]
        return found

    barrier = pltpu.get_barrier_semaphore()
    loads = [
        pltpu.make_async_copy(src, dst, in_sem.at[i])
        for i, (src, dst) in enumerate(
            [
                (res_hbm, res),
                (agg_hbm, agg),
                (inv_hbm, inv),
                (hvec_hbm, hvec),
                (hval_hbm, hval),
                (ztab_hbm, ztab),
                (zval_hbm, zval),
            ]
        )
    ]
    for load in loads:
        load.start()
    corner_dy = (1,) if members == 2 else (1, -1)
    around = [(1, 0), (-1, 0), (0, 1)] + [(0, -1)] * (members > 2)
    around += [(dx, dy) for dx in (1, -1) for dy in corner_dy]
    partners = peers() if direct else [shifted(dx, dy) for dx, dy in around]
    for device in partners:
        pl.semaphore_signal(barrier, inc=1, device_id=device, device_id_type=MESH)
    hpad[...] = jnp.zeros_like(hpad)
    apad[...] = jnp.zeros_like(apad)

    wide = 2 * MAIN
    lane = iota((1, wide), 1)
    row = iota((TAIL, wide), 0)
    eye = hot(iota((TAIL, 128), 0) == iota((TAIL, 128), 1))
    px, py = point_index(lane)
    ma, mb = mode_index(lane)
    px, py, ma, mb = [hot(i == row) for i in (px, py, ma, mb)]
    stacked = count_z * EXTENT
    mode = iota((1, modes_z), 1)
    mode_layer = mode // EXTENT
    mode_inner = mode - EXTENT * mode_layer
    tiled = hot(mode_inner == iota((EXTENT, modes_z), 0))
    zz = iota((span_z, stacked), 0)
    layer = iota((1, stacked), 1) % count_z
    inner = iota((1, stacked), 1) // count_z
    band = hot(zz == SPAN * layer - 1 + inner)
    near = hot((high(zz) == layer) & (inner == low(zz) + 1))
    eye_z = hot(iota((modes_z, modes_z), 0) == iota((modes_z, modes_z), 1))
    row8 = iota((8, span_z), 0)
    spread = hot(high(iota((count_z, span_z), 1)) == iota((count_z, span_z), 0))
    for load in loads[1:]:
        load.wait()

    if direct:
        half = inv.shape[1]
        labels = dot(agg[0].astype(F32), spread.astype(F32))
        row_id = iota((2 * half, span_z), 0).astype(F32)
        member_of = [(labels[j : j + 1, :] == row_id).astype(F32) for j in range(count_y)]
        downward = hot(high(iota((span_z, count_z), 0)) == iota((span_z, count_z), 1))
        upright = dot_t(downward.astype(F32), agg[0].astype(F32))
        lane_id = iota((span_z, 2 * half), 1).astype(F32)
        owned = jnp.concatenate(
            [hot(upright[:, j : j + 1] == lane_id) for j in range(count_y)], axis=0
        )
        apad[:, 0:half] = inv[...]
    diag = choose(ztab[...].reshape(stacked, EXTENT), tiled)
    diag = jnp.where(mode_layer == iota((stacked, modes_z), 0) % count_z, diag, 0.0)
    hi, lo = split(place(band, diag))
    zfwd[0:span_z, :] = hi
    zfwd[span_z : 2 * span_z, :] = lo
    zfwd[2 * span_z : 3 * span_z, :] = hi
    hi, lo = split(turn(eye_z, place(near, diag)))
    zbwd[:, 0:span_z] = hi
    zbwd[:, span_z : 2 * span_z] = lo

    levels = dot(zval[...], tiled.astype(F32))
    level_own = mode_layer == iota((count_z, modes_z), 0)
    levels = jnp.sum(jnp.where(level_own, levels, 0.0), axis=0, keepdims=True)
    upright_eye = (iota((TAIL, EXTENT), 0) == iota((TAIL, EXTENT), 1)).astype(F32)
    columns = dot_t(upright_eye, hval[...])
    first = jnp.broadcast_to(columns[:, 0:1], (TAIL, modes_z))
    second = columns[:, 1:2] + levels
    body = first[:EXTENT][:, None, :] + second[:SPAN][None, :, :]
    recip[0 : EXTENT * SPAN, :] = 1.0 / body.reshape(EXTENT * SPAN, modes_z)
    for side in range(2):
        rows = slice(EXTENT * SPAN + side * TAIL, EXTENT * SPAN + (side + 1) * TAIL)
        recip[rows, :] = 1.0 / (first + second[SPAN + side : SPAN + side + 1, :])

    loads[0].wait()

    for v in range(vectors):
        ysend[0, v] = res[v, :, span_y - 1, :]
        ysend[1, v] = res[v, :, 0, :]
    for cx in range(2):
        for cy in range(2):
            for v in range(vectors):
                row = cx * 4 + cy * 2 + v
                y_at = (span_y - 1) * cy
                csend[row : row + 1, :] = res[v, (SPAN - 1) * cx, y_at : y_at + 1, :]

    if direct:
        sums = []
        for j in range(count_y):
            placed = jnp.zeros((8, span_z), F32)
            for v in range(vectors):
                tot = jnp.sum(res[v, :, j * SPAN : (j + 1) * SPAN, :], axis=0)
                tot = jnp.sum(tot, axis=0, keepdims=True)
                placed = placed + jnp.where((row8 & 3) == v, tot, 0.0)
            sums.append(placed)
        hi, lo = split(jnp.concatenate(sums, axis=1))
        rhs = WEIGHT * (bdot(hi, owned) + bdot(lo, owned))
        lane8 = iota((8, 2 * half), 1)
        rhs = jnp.where(row8 < 4, pltpu.roll(rhs, half, 1), rhs)
        mine = apad[...] + jnp.where(lane8 < half, 0.0, rhs)
        msg[me] = mine
        box[...] = mine

    halo = []

    def send(src, dst, dx, dy):
        i = len(halo)
        copy = pltpu.make_async_remote_copy(
            src_ref=src,
            dst_ref=dst,
            send_sem=halo_send.at[i],
            recv_sem=halo_recv.at[i],
            device_id=shifted(dx, dy),
            device_id_type=MESH,
        )
        halo.append(copy)

    send(res.at[:, SPAN - 1], xrecv.at[0], 1, 0)
    send(res.at[:, 0], xrecv.at[1], -1, 0)
    for ix, dx in enumerate((1, -1)):
        for iy, dy in enumerate(corner_dy):
            send(csend, crecv.at[ix, iy], dx, dy)
    send(ysend.at[0], yrecv.at[0], 0, 1)
    send(ysend.at[1], yrecv.at[1], 0, -1)

    pl.semaphore_wait(barrier, len(partners))
    for copy in halo:
        copy.start()
    if direct:
        shares = [
            pltpu.make_async_remote_copy(
                src_ref=box,
                dst_ref=msg.at[me],
                send_sem=all_send,
                recv_sem=all_recv,
                device_id=device,
                device_id_type=MESH,
            )
            for device in partners
        ]
        for copy in shares:
            copy.start()

    hpad[0, 0:EXTENT, 0:EXTENT] = hvec[:, 0, :]
    hpad[1, 0:EXTENT, 0:EXTENT] = hvec[:, 1, :]
    xe = choose(turn(eye, hpad[0]), px)
    ye = choose(turn(eye, hpad[1]), py)
    body = xe[:EXTENT][:, None, :] * ye[:SPAN][None, :, :]
    table = jnp.concatenate(
        [
            body.reshape(EXTENT * SPAN, wide),
            xe * ye[SPAN : SPAN + 1, :],
            xe * ye[SPAN + 1 : SPAN + 2, :],
        ],
        axis=0,
    )
    store_split(fwd, table)
    xb = choose(hpad[0, 1 : SPAN + 1, 0:TAIL], ma)
    yb = choose(hpad[1, 1 : SPAN + 1, 0:TAIL], mb)
    store_split(bwd, (xb[:, None, :] * yb[None, :, :]).reshape(MAIN, wide))

    for v in range(vectors):
        field = jnp.concatenate(
            [
                res[v, :, j * SPAN : (j + 1) * SPAN, :].reshape(MAIN, span_z)
                for j in range(count_y)
            ],
            axis=1,
        )
        hi, lo = split(field)
        part[v] = bdot(fwd[:, 0 : 3 * MAIN], jnp.concatenate([hi, lo, hi], axis=0))

    for copy in halo:
        copy.wait_recv()

    rim_row = iota((8, span_z), 0)
    solved = []
    for v in range(vectors):
        rests = []
        for j in range(count_y):
            rows = slice(j * SPAN, (j + 1) * SPAN)
            pieces = [xrecv[0, v, rows, :], xrecv[1, v, rows, :]]
            for side in range(2):
                at = j * SPAN - 1 if side == 0 else (j + 1) * SPAN
                if 0 <= at < span_y:
                    pieces.append(res[v, :, at, :])
                    before = xrecv[0, v, at : at + 1, :]
                    after = xrecv[1, v, at : at + 1, :]
                else:
                    pieces.append(yrecv[side, v])
                    iy = 0 if members == 2 else side
                    cy = 1 - side
                    r0, r1 = 4 + cy * 2 + v, cy * 2 + v
                    before = crecv[0, iy, r0 : r0 + 1, :]
                    after = crecv[1, iy, r1 : r1 + 1, :]
                pieces.append(
                    jnp.where(rim_row == 0, before, jnp.where(rim_row == 1, after, 0.0))
                )
            rests.append(jnp.concatenate(pieces, axis=0))
        hi, lo = split(jnp.concatenate(rests, axis=1))
        hat = part[v] + bdot(fwd[:, 3 * MAIN :][:, : 3 * REST], jnp.concatenate([hi, lo, hi], axis=0))
        stack = jnp.concatenate(
            [hat[:, j * span_z : (j + 1) * span_z] for j in range(count_y)], axis=0
        )
        hi, lo = split(stack)
        spectral = bdot(jnp.concatenate([hi, hi, lo], axis=1), zfwd[...])
        weight = recip[...]
        spectral = spectral * jnp.concatenate([weight] * count_y, axis=0)
        hi, lo = split(spectral)
        both = bdot(hi, zbwd[...])
        back = both[:, :span_z] + both[:, span_z:] + bdot(lo, zbwd[:, 0:span_z])
        solved.append(
            jnp.concatenate([back[j * ROWS : (j + 1) * ROWS] for j in range(count_y)], axis=1)
        )

    updates = []
    if direct:
        everyone = msg.at[pl.ds(0, total - 1)]
        pltpu.make_async_copy(everyone, everyone, all_recv).wait()
        blocks = msg[...]
        whole = pltpu.roll(jnp.sum(blocks, axis=0), half, 1)
        whole = jnp.where(lane8 < half, whole, 0.0)
        blocks = blocks.reshape(groups, members, 8, 2 * half)
        for v in range(vectors):
            terms = jnp.zeros((groups, 8, 2 * half), F32)
            for part_m in range(members):
                at = 4 * part_m + v
                terms = terms + blocks[:, part_m] * whole[at : at + 1, :][None]
            answer = jnp.sum(terms.reshape(groups * 8, 2 * half), axis=1, keepdims=True)
            updates.append(
                [
                    WEIGHT * jnp.sum(answer * member_of[j], axis=0, keepdims=True)
                    for j in range(count_y)
                ]
            )

    stores = []
    for v in range(vectors):
        hi, lo = split(solved[v])
        main_part = jnp.concatenate([hi[:MAIN], lo[:MAIN], hi[:MAIN]], axis=0)
        rest_part = jnp.concatenate([hi[MAIN:], lo[MAIN:], hi[MAIN:]], axis=0)
        for piece_x in range(2):
            rows = slice(piece_x * MAIN // 2, (piece_x + 1) * MAIN // 2)
            points = slice(piece_x * SPAN // 2, (piece_x + 1) * SPAN // 2)
            result = bdot(bwd[rows, 0 : 3 * MAIN], main_part) + bdot(
                bwd[rows, 3 * MAIN :][:, : 3 * REST], rest_part
            )
            for j in range(count_y):
                piece = result[:, j * span_z : (j + 1) * span_z]
                if direct:
                    piece = piece + updates[v][j]
                out[v, points, j * SPAN : (j + 1) * SPAN, :] = piece.reshape(
                    SPAN // 2, SPAN, span_z
                )
            store = pltpu.make_async_copy(
                out.at[v, points], out_hbm.at[v, points], out_sem.at[2 * v + piece_x]
            )
            store.start()
            stores.append(store)

    for copy in halo:
        copy.wait_send()
    if direct:
        pltpu.make_async_copy(everyone, everyone, all_send).wait()
    for store in stores:
        store.wait()


def on_device(
    residual,
    horiz_vectors,
    horiz_values,
    upward_eigen_tables,
    upward_eigen_values,
    aggregate_map,
    coarse_inverse,
):
    groups = lax.axis_size("group")
    members = lax.axis_size("member")
    vectors, points_x, span_y, span_z = residual.shape
    count_y = span_y // SPAN
    count_z = span_z // SPAN
    total = groups * members
    rows, cols = coarse_inverse.shape
    direct = total <= 64 and members == 2 and rows == 8 and cols == 64 and groups * 8 == 128
    operands = (
        residual,
        jnp.transpose(horiz_vectors, (1, 0, 2)),
        horiz_values,
        jnp.transpose(upward_eigen_tables, (1, 0, 2)),
        upward_eigen_values,
        aggregate_map,
        coarse_inverse,
    )
    corners = 1 if members == 2 else 2
    halos = 4 + 2 * corners
    dma = pltpu.SemaphoreType.DMA
    scratch = [pltpu.VMEM(a.shape, a.dtype) for a in operands]
    scratch += [
        pltpu.VMEM(residual.shape, F32),
        pltpu.VMEM((2, TAIL, 128), F32),
        pltpu.VMEM((8, 128), F32),
        pltpu.VMEM((2, vectors, SPAN, span_z), F32),
        pltpu.VMEM((8, span_z), F32),
        pltpu.VMEM((2, vectors, span_y, span_z), F32),
        pltpu.VMEM((2, vectors, SPAN, span_z), F32),
        pltpu.VMEM((2, corners, 8, span_z), F32),
        pltpu.VMEM((total if direct else 1, 8, 128), F32),
        pltpu.VMEM((8, 128), F32),
        pltpu.VMEM((ROWS, 4 * MAIN), BF16),
        pltpu.VMEM((MAIN, 4 * MAIN), BF16),
        pltpu.VMEM((ROWS, count_z * EXTENT), F32),
        pltpu.VMEM((3 * span_z, count_z * EXTENT), BF16),
        pltpu.VMEM((count_z * EXTENT, 2 * span_z), BF16),
        pltpu.VMEM((vectors, ROWS, count_y * span_z), F32),
        dma((len(operands),)),
        dma((2 * vectors,)),
        dma((halos,)),
        dma((halos,)),
        dma,
        dma,
    ]
    result = pl.pallas_call(
        functools.partial(kernel, groups, members, direct),
        out_shape=jax.ShapeDtypeStruct(residual.shape, F32),
        in_specs=[pl.BlockSpec(memory_space=pltpu.HBM)] * len(operands),
        out_specs=pl.BlockSpec(memory_space=pl.ANY),
        scratch_shapes=scratch,
        compiler_params=pltpu.CompilerParams(
            collective_id=0, has_side_effects=True, vmem_limit_bytes=40 * 1024 * 1024
        ),
        cost_estimate=pl.CostEstimate(
            flops=2 * 10**9, bytes_accessed=2**20, transcendentals=0
        ),
    )(*operands)
    if direct:
        return result
    totals = residual.reshape(vectors, SPAN, count_y, SPAN, count_z, SPAN).sum(axis=(1, 3, 5))
    labels = aggregate_map.reshape(-1)
    partial_rhs = WEIGHT * jax.ops.segment_sum(
        totals.reshape(vectors, -1).T, labels, num_segments=rows * groups
    ).T
    whole_rhs = lax.psum(partial_rhs, ("group", "member"))
    share = lax.dynamic_slice_in_dim(whole_rhs, lax.axis_index("member") * cols, cols, 1)
    row_values = lax.psum(dot(share, coarse_inverse.T), "member")
    coarse = lax.all_gather(row_values, "group", axis=1, tiled=True)
    update = WEIGHT * jnp.take(coarse, labels, axis=1)
    update = update.reshape(vectors, 1, count_y, 1, count_z, 1)
    split_up = (vectors, SPAN, count_y, SPAN, count_z, SPAN)
    return (result.reshape(split_up) + update).reshape(residual.shape)


def solution(mesh):
    in_specs = (
        P(None, "group", "member", None),
        P(),
        P(),
        P(),
        P(),
        P("group", "member", None),
        P("group", "member"),
    )
    out_specs = P(None, "group", "member", None)
    return jax.shard_map(
        on_device, mesh=mesh, in_specs=in_specs, out_specs=out_specs, check_vma=False
    )
```
